256 devices in a mesh: tm: 16 (over x_lo, y, core), dp: 16 (over z, x_hi).
Axes of the slice: x: 4 (x_hi: 2, x_lo: 2; x = x_hi * 2 + x_lo), y: 4, z: 8, core: 2. Of those that a mesh axis runs over, the one named last changes fastest.
Arguments:
- tokens: bfloat16 [2, 32, 1024, 1536], P(None, 'tm', 'dp'), may hold values from -6 to 6
- space_gain: float32 [1536], replicated, may hold values from 0.25 to 1.75
- spatial_project: bfloat16 [1536, 2304], P('dp'), may hold values from -0.8164966 to 0.8164966
- spatial_output: bfloat16 [768, 1536], P('dp'), may hold values from -0.21875 to 0.21875
- time_gain: float32 [1536], replicated, may hold values from 0.25 to 1.75
- temporal_project: bfloat16 [1536, 2304], P('dp'), may hold values from -0.8164966 to 0.8164966
Outputs:
- spatial_branch: bfloat16 [2, 32, 1024, 1536], P(None, 'tm', 'dp')
- temporal_context: bfloat16 [2, 32, 1024, 768], P(None, 'tm', 'dp')
The draws below stay inside these ranges and needn't reach their ends.
All inputs are finite; a program needn't handle non-finite values.
Results may differ from the reference program's by a relative error of at most 0.02.
Values may be sent and summed in bfloat16 or wider, within the bound.
No kernel may reach another device: no remote copies, remote signals or barrier semaphores. Data moves between devices by JAX's collectives and lax.ppermute only.
A program may use at most 128 MiB of HBM per device.

```python
import math
import jax
import jax.numpy as jnp
from jax import lax

D = 1536
HEADS = 8
HSIZE = 96
BATCH = 2
INNER = 768
FRAMES = 32
TOKF = 1024


def attention_columns(key, lowest, highest):
    key_query, key_keys, key_values, key_strength = jax.random.split(key, 4)
    strength = jnp.exp(jax.random.uniform(key_strength, (HEADS,), jnp.float32, jnp.log(lowest), jnp.log(highest)))
    factor = jnp.repeat(strength, HSIZE) * D ** (-0.5)
    query = jnp.clip(jax.random.normal(key_query, (D, INNER), jnp.float32), -4.0, 4.0) * factor
    noise = jnp.clip(jax.random.normal(key_keys, (D, INNER), jnp.float32), -4.0, 4.0) * factor
    keys = noise
    values = jnp.clip(jax.random.normal(key_values, (D, INNER), jnp.float32), -4.0, 4.0) * D ** (-0.5)
    return jnp.concatenate([query, keys, values], axis=1).astype(jnp.bfloat16)


def draw_spatial_project(key, part):
    key = jax.random.fold_in(key, 11)
    return attention_columns(key, 1.2, 2.0)


def draw_temporal_project(key, part):
    key = jax.random.fold_in(key, 23)
    return attention_columns(key, 1.2, 2.0)


def block_levels(stream_key, dims, pieces, low, high):
    loudness = 1.0
    for axis_at, shards_of in pieces:
        draws = jax.random.uniform(jax.random.fold_in(jax.random.fold_in(stream_key, 6), axis_at), (shards_of,), jnp.float32, low / len(pieces), high / len(pieces))
        loudness = loudness * jnp.repeat(jnp.exp(draws), dims[axis_at] // shards_of).reshape((-1,) + (1,) * (len(dims) - 1 - axis_at))
    return loudness


def gaussian(key, extent, spread, reach, pieces=(), dtype=jnp.bfloat16):
    values = spread * jax.random.normal(key, extent, jnp.float32)
    if pieces:
        values = values * block_levels(key, extent, pieces, -0.22, 0.18)
    return jnp.clip(values, -reach, reach).astype(dtype)


def setup_inputs(seed: int = 0) -> dict:
    streams_of = jax.random.split(jax.random.key(seed), 7)
    return {
        "tokens": gaussian(streams_of[0], (BATCH, FRAMES, TOKF, D), 1.0, 6.0, ((1, 16), (2, 16))),
        "space_gain": jnp.clip(1.0 + 0.15 * jax.random.normal(streams_of[1], (D,), jnp.float32), 0.25, 1.75),
        "spatial_project": draw_spatial_project(jax.random.fold_in(streams_of[6], 71), 0),
        "spatial_output": gaussian(streams_of[3], (INNER, D), INNER ** -0.5, 0.21875, ((0, 16),)),
        "time_gain": jnp.clip(1.0 + 0.15 * jax.random.normal(streams_of[4], (D,), jnp.float32), 0.25, 1.75),
        "temporal_project": draw_temporal_project(jax.random.fold_in(streams_of[6], 71), 0),
    }


EPSILON = 1e-05

def normalize(values, gain):
    factor = lax.rsqrt(lax.optimization_barrier(jnp.mean(values * values, axis=-1, keepdims=True)) + EPSILON)
    return (values * factor * gain.astype(jnp.float32)).astype(jnp.bfloat16)

def temporal_attend(projected, inner, hsize):
    batch, frames, columns, _ = projected.shape
    query = projected[..., :inner].astype(jnp.float32).reshape(batch, frames, columns, HEADS, hsize)
    keys = projected[..., inner:2 * inner].astype(jnp.float32).reshape(batch, frames, columns, HEADS, hsize)
    values = projected[..., 2 * inner:].astype(jnp.float32).reshape(batch, frames, columns, HEADS, hsize)
    scores = jnp.einsum('bfnhd,bgnhd->bnhfg', query, keys) * (1.0 / math.sqrt(hsize))
    causal = lax.broadcasted_iota(jnp.int32, (frames, frames), 0) >= lax.broadcasted_iota(jnp.int32, (frames, frames), 1)
    scores = jnp.where(causal, scores, -jnp.inf)
    peak = lax.optimization_barrier(jnp.max(scores, axis=-1, keepdims=True))
    weights = jnp.exp(scores - peak)
    summed = lax.optimization_barrier(jnp.sum(weights, axis=-1))
    rounded = lax.optimization_barrier(weights.astype(jnp.bfloat16)).astype(jnp.float32)
    context = jnp.einsum('bnhfg,bgnhd->bfnhd', rounded, values)
    context = context / jnp.transpose(summed, (0, 3, 1, 2))[..., None]
    return context.astype(jnp.bfloat16).reshape(batch, frames, columns, inner)

def reference(tokens, space_gain, spatial_project, spatial_output, time_gain, temporal_project):
    batch, frames, per_frame, width = tokens.shape
    inner = spatial_project.shape[1] // 3
    hsize = inner // HEADS
    factor = 1.0 / math.sqrt(hsize)
    normed = normalize(tokens.astype(jnp.float32), space_gain).reshape(-1, width)
    projected = jnp.dot(normed, spatial_project, preferred_element_type=jnp.float32).astype(jnp.bfloat16)
    projected = projected.reshape(batch * frames, per_frame, 3 * inner)

    def one_frame(block):
        query = block[:, :inner].astype(jnp.float32).reshape(per_frame, HEADS, hsize)
        keys = block[:, inner:2 * inner].astype(jnp.float32).reshape(per_frame, HEADS, hsize)
        values = block[:, 2 * inner:].astype(jnp.float32).reshape(per_frame, HEADS, hsize)
        scores = jnp.einsum('qhd,khd->hqk', query, keys) * factor
        peak = lax.optimization_barrier(jnp.max(scores, axis=-1, keepdims=True))
        weights = jnp.exp(scores - peak)
        summed = lax.optimization_barrier(jnp.sum(weights, axis=-1))
        rounded = lax.optimization_barrier(weights.astype(jnp.bfloat16)).astype(jnp.float32)
        context = jnp.einsum('hqk,khd->qhd', rounded, values) / jnp.transpose(summed)[:, :, None]
        return context.astype(jnp.bfloat16).reshape(per_frame, inner)
    context = lax.map(one_frame, projected).reshape(-1, inner)
    branch = jnp.dot(context, spatial_output, preferred_element_type=jnp.float32).astype(jnp.bfloat16)
    branch = branch.reshape(batch, frames, per_frame, width)
    mixed = tokens.astype(jnp.float32) + branch.astype(jnp.float32)
    normed_time = normalize(mixed, time_gain).reshape(-1, width)
    time_proj = jnp.dot(normed_time, temporal_project, preferred_element_type=jnp.float32).astype(jnp.bfloat16)
    time_proj = time_proj.reshape(batch, frames, per_frame, 3 * inner)
    return (branch, temporal_attend(time_proj, inner, hsize))
```

```python
import math

import jax
import jax.numpy as jnp
from jax import lax
from jax.experimental import pallas as pl
from jax.experimental.pallas import tpu as pltpu
from jax.sharding import Mesh
from jax.sharding import PartitionSpec as P

HEADS = 8
HSIZE = 96
WIDTH = 1536
INNER = 768
HALF = INNER // 2
EPSILON = 1e-05
SCALE = math.log2(math.e) / math.sqrt(HSIZE)
TM = ("x_lo", "y", "core")
DP = ("z", "x_hi")
BF16 = jnp.bfloat16
F32 = jnp.float32


def params():
    return pltpu.CompilerParams(vmem_limit_bytes=56 * 1024 * 1024)


def dot(a, b):
    return jnp.dot(a, b, preferred_element_type=F32)


def dot_nt(a, b):
    return lax.dot_general(a, b, (((1,), (1,)), ((), ())), preferred_element_type=F32)


def shuffle(size, rows):
    column = lax.broadcasted_iota(jnp.int32, (1, size), 1)
    per = 16 * rows
    source = (column % per) // rows * per + column // per * rows + column % rows
    return (lax.broadcasted_iota(jnp.int32, (size, size), 0) == source).astype(BF16)


def norm_kernel(x_ref, gain_ref, shuffle_ref, out_ref):
    x = x_ref[...].astype(F32)
    factor = lax.rsqrt(jnp.mean(x * x, axis=-1, keepdims=True) + EPSILON)
    normed = (x * factor * gain_ref[...]).astype(BF16)
    out_ref[...] = dot(normed, shuffle_ref[...]).astype(BF16)


def project_kernel(own_ref, other_ref, w_ref, q_ref, kv_ref):
    step = pl.program_id(0)
    w = w_ref[...].reshape(WIDTH, HALF)
    rows = own_ref.shape[0]
    first = dot(own_ref[...], w).astype(BF16)
    second = dot(other_ref[...], w).astype(BF16)

    @pl.when(step == 0)
    def _():
        q_ref[:rows] = first
        q_ref[rows:] = second

    @pl.when(step > 0)
    def _():
        kv_ref[0, :rows] = first
        kv_ref[0, rows:] = second


def spatial_kernel(xh_ref, q_ref, kv_ref, kvo_ref, out_ref):
    rows = q_ref.shape[0]
    for h in range(HEADS // 2):
        lanes = slice(h * HSIZE, (h + 1) * HSIZE)
        q = q_ref[:, lanes]
        s0 = dot_nt(q, kv_ref[0, :, lanes])
        s1 = dot_nt(q, kvo_ref[0, :, lanes])
        peak = jnp.maximum(
            jnp.max(s0, axis=-1, keepdims=True), jnp.max(s1, axis=-1, keepdims=True)
        )
        e0 = jnp.exp2((s0 - peak) * SCALE)
        e1 = jnp.exp2((s1 - peak) * SCALE)
        summed = jnp.sum(e0, axis=-1, keepdims=True) + jnp.sum(e1, axis=-1, keepdims=True)
        acc = dot(e0.astype(BF16), kv_ref[1, :, lanes]) + dot(e1.astype(BF16), kvo_ref[1, :, lanes])
        out_ref[:, 0, :, lanes] = (acc / summed).astype(BF16).reshape(rows // 32, 32, HSIZE)


def output_kernel(ctx_ref, tok_ref, w_ref, gain_ref, sh3_ref, sh6_ref, branch_ref, out_ref):
    rows = tok_ref.shape[0]
    ctx = jnp.concatenate(
        [ctx_ref[:, 0].reshape(rows, HALF), ctx_ref[:, 1].reshape(rows, HALF)], axis=1
    )
    ctx = dot(ctx, sh3_ref[...]).astype(BF16)
    mixed = []
    total = jnp.zeros((rows, 1), F32)
    for cb in range(4):
        lanes = slice(cb * HALF, (cb + 1) * HALF)
        w = w_ref[:, cb * 48 : (cb + 1) * 48, :].reshape(INNER, HALF)
        branch = dot(ctx, w).astype(BF16)
        branch_ref[:, lanes] = branch
        mix = tok_ref[:, lanes].astype(F32) + branch.astype(F32)
        mixed.append(mix)
        total += jnp.sum(mix * mix, axis=-1, keepdims=True)
    factor = lax.rsqrt(total * (1.0 / WIDTH) + EPSILON)
    target = lax.broadcasted_iota(jnp.int32, (rows, rows), 0)
    source = (target % 32) // 4 * 32 + target // 32 * 4 + target % 4
    swap = (lax.broadcasted_iota(jnp.int32, (rows, rows), 1) == source).astype(BF16)
    normed = jnp.concatenate(
        [
            (mix * factor * gain_ref[:, cb * HALF : (cb + 1) * HALF]).astype(BF16)
            for cb, mix in enumerate(mixed)
        ],
        axis=1,
    )
    normed = dot(swap, normed).astype(BF16)
    out_ref[...] = dot(normed, sh6_ref[...]).astype(BF16)


def temporal_kernel(x_ref, w_ref, out_ref, q_scr, k_scr):
    step = pl.program_id(0)
    rows = x_ref.shape[0]
    projected = dot(x_ref[...], w_ref[...].reshape(WIDTH, HALF)).astype(BF16)
    kind = step % 3

    @pl.when(kind == 0)
    def _():
        q_scr[...] = projected

    @pl.when(kind == 1)
    def _():
        k_scr[...] = projected

    @pl.when(kind == 2)
    def _():
        r = lax.broadcasted_iota(jnp.int32, (rows, rows), 0)
        s = lax.broadcasted_iota(jnp.int32, (rows, rows), 1)
        same = (r % 4 == s % 4) & ((r // 8) % 2 == (s // 8) % 2)
        seen = (r // 16) * 2 + (r // 4) % 2 >= (s // 16) * 2 + (s // 4) % 2
        mask = same & seen
        for h in range(HEADS // 2):
            lanes = slice(h * HSIZE, (h + 1) * HSIZE)
            scores = dot_nt(q_scr[:, lanes], k_scr[:, lanes])
            scores = jnp.where(mask, scores, -jnp.inf)
            peak = jnp.max(scores, axis=-1, keepdims=True)
            weights = jnp.exp2((scores - peak) * SCALE)
            summed = jnp.sum(weights, axis=-1, keepdims=True)
            acc = dot(weights.astype(BF16), projected[:, lanes])
            out_ref[:, lanes] = (acc / summed).astype(BF16)


def whole(shape):
    return pl.BlockSpec(shape, lambda *_: (0,) * len(shape))


def pick(first, a, b, axis):
    return jnp.where(first, jnp.concatenate([a, b], axis), jnp.concatenate([b, a], axis))


def per_device(tokens, space_gain, spatial_project, spatial_output, time_gain, temporal_project):
    core = lax.axis_index("core")
    x_hi = lax.axis_index("x_hi")
    tm = lax.axis_index(TM)
    swap = [(0, 1), (1, 0)]
    sh6 = shuffle(WIDTH, 6)
    sh3 = shuffle(INNER, 3)

    wq = lax.dynamic_slice_in_dim(spatial_project, tm * 6, 6, 0)
    wq = wq.reshape(6, 3, 2, HALF).transpose(2, 1, 0, 3).reshape(2, 18, HALF)
    wo = lax.dynamic_slice_in_dim(spatial_output, tm * 3, 3, 0)
    wo = wo.reshape(3, 4, HALF).transpose(1, 0, 2).reshape(12, HALF)
    wt = lax.dynamic_slice_in_dim(temporal_project, tm * 6, 6, 0)
    wt = wt.reshape(6, 6, HALF).transpose(1, 0, 2).reshape(36, HALF)
    chunk = jnp.stack([jnp.concatenate([wo, wq[i], wt], 0) for i in range(2)])
    chunk = jnp.broadcast_to(chunk[None], (8, 2, 66, HALF)).reshape(16, 66, HALF)
    got = lax.all_to_all(chunk, DP, 0, 0, tiled=True)
    w1 = jnp.concatenate(
        [
            got[:, :12].reshape(16, 4, 3, HALF).transpose(1, 0, 2, 3).reshape(192, HALF),
            got[:, 12:30].reshape(16, 3, 6, HALF).transpose(1, 0, 2, 3).reshape(288, HALF),
        ],
        0,
    )
    w2 = got[:, 30:].reshape(16, 6, 6, HALF).transpose(1, 0, 2, 3).reshape(576, HALF)
    w1 = lax.all_gather(w1, TM, axis=0, tiled=False)
    w2 = lax.all_gather(w2, TM, axis=0, tiled=False)

    halves = tokens.reshape(4, 2, 32, WIDTH)
    keep = lax.dynamic_index_in_dim(halves, core, 1, keepdims=False)
    send = lax.dynamic_index_in_dim(halves, 1 - core, 1, keepdims=False)
    frames = pick(core == 0, keep, lax.ppermute(send, "core", swap), 0).reshape(256, WIDTH)
    normed = pl.pallas_call(
        norm_kernel,
        out_shape=jax.ShapeDtypeStruct((256, WIDTH), BF16),
        compiler_params=params(),
        name="space_norm",
    )(frames, space_gain.reshape(1, WIDTH), sh6)
    own = lax.all_to_all(normed.reshape(8, 32, WIDTH), "z", 0, 0, tiled=True)
    other = lax.ppermute(own, "x_hi", swap)
    q, kv = pl.pallas_call(
        project_kernel,
        grid=(3,),
        in_specs=[
            whole((256, WIDTH)),
            whole((256, WIDTH)),
            pl.BlockSpec((16, 96, HALF), lambda i: (0, i + 2, 0)),
        ],
        out_specs=[
            whole((512, HALF)),
            pl.BlockSpec((1, 512, HALF), lambda i: (jnp.maximum(i - 1, 0), 0, 0)),
        ],
        out_shape=[
            jax.ShapeDtypeStruct((512, HALF), BF16),
            jax.ShapeDtypeStruct((2, 512, HALF), BF16),
        ],
        compiler_params=params(),
        name="space_project",
    )(own.reshape(256, WIDTH), other.reshape(256, WIDTH), w1)
    kvo = lax.ppermute(kv, "core", swap)
    ctx = pl.pallas_call(
        spatial_kernel,
        grid_spec=pltpu.PrefetchScalarGridSpec(
            num_scalar_prefetch=1,
            grid=(2, 2),
            in_specs=[
                pl.BlockSpec((128, HALF), lambda i, j, xh: (i * 2 + j, 0)),
                whole((2, 512, HALF)),
                whole((2, 512, HALF)),
            ],
            out_specs=pl.BlockSpec(
                (4, 1, 32, HALF), lambda i, j, xh: (j, (i + xh[0]) % 2, 0, 0)
            ),
        ),
        out_shape=jax.ShapeDtypeStruct((8, 2, 32, HALF), BF16),
        compiler_params=params(),
        name="space_attend",
    )(x_hi.reshape(1).astype(jnp.int32), q, kv, kvo)
    ctx = lax.all_to_all(ctx.reshape(16, 32, HALF), DP, 0, 0, tiled=True)
    branch, normed_time = pl.pallas_call(
        output_kernel,
        grid=(1,),
        in_specs=[
            whole((8, 2, 32, HALF)),
            whole((256, WIDTH)),
            whole((16, 192, HALF)),
            whole((1, WIDTH)),
            whole((INNER, INNER)),
            whole((WIDTH, WIDTH)),
        ],
        out_specs=[whole((256, WIDTH)), whole((256, WIDTH))],
        out_shape=[
            jax.ShapeDtypeStruct((256, WIDTH), BF16),
            jax.ShapeDtypeStruct((256, WIDTH), BF16),
        ],
        compiler_params=params(),
        name="space_output",
    )(ctx.reshape(8, 2, 32, HALF), frames, w1, time_gain.reshape(1, WIDTH), sh3, sh6)
    branch = branch.reshape(8, 32, WIDTH)
    mine = lax.dynamic_slice_in_dim(branch, core * 4, 4, 0)
    theirs = lax.dynamic_slice_in_dim(branch, (1 - core) * 4, 4, 0)
    back = lax.ppermute(theirs, "core", swap)
    branch = pick(core == 0, mine[:, None], back[:, None], 1).reshape(tokens.shape)

    columns = lax.all_to_all(normed_time.reshape(8, 32, WIDTH), TM[:2], 0, 0, tiled=True)
    context = pl.pallas_call(
        temporal_kernel,
        grid=(6,),
        in_specs=[
            whole((256, WIDTH)),
            pl.BlockSpec((16, 96, HALF), lambda i: (0, i % 3 * 2 + i // 3, 0)),
        ],
        out_specs=pl.BlockSpec((256, HALF), lambda i: (0, i // 3)),
        out_shape=jax.ShapeDtypeStruct((256, INNER), BF16),
        scratch_shapes=[pltpu.VMEM((256, HALF), BF16), pltpu.VMEM((256, HALF), BF16)],
        compiler_params=params(),
        name="time_attend",
    )(columns.reshape(256, WIDTH), w2)
    context = lax.all_to_all(context.reshape(16, 16, INNER), TM, 0, 0, tiled=True)
    context = context.reshape(8, 2, 2, 2, 4, INNER).transpose(2, 3, 1, 0, 4, 5)
    return branch, context.reshape(2, 2, 64, INNER)


def solution(mesh):
    fine = Mesh(mesh.devices.reshape(2, 4, 2, 8, 2), TM + DP)
    in_specs = (P(None, TM, DP, None), P(), P(DP, None), P(DP, None), P(), P(DP, None))
    out_specs = (P(None, TM, DP, None), P(None, TM, DP, None))
    return jax.shard_map(
        per_device, mesh=fine, in_specs=in_specs, out_specs=out_specs, check_vma=False
    )
```

```python
import functools
import math

import jax
import jax.numpy as jnp
from jax import lax
from jax.experimental import pallas as pl
from jax.experimental.pallas import tpu as pltpu
from jax.sharding import Mesh
from jax.sharding import PartitionSpec as P

HEADS = 8
HSIZE = 96
WIDTH = 1536
INNER = 768
HALF = INNER // 2
EPSILON = 1e-05
SCALE = math.log2(math.e) / math.sqrt(HSIZE)
TM = ("x_lo", "y", "core")
DP = ("z", "x_hi")
BF16 = jnp.bfloat16
F32 = jnp.float32


def params():
    return pltpu.CompilerParams(vmem_limit_bytes=56 * 1024 * 1024)


def dot(a, b):
    return jnp.dot(a, b, preferred_element_type=F32)


def dot_nt(a, b):
    return lax.dot_general(a, b, (((1,), (1,)), ((), ())), preferred_element_type=F32)


def shuffle(size, rows):
    column = lax.broadcasted_iota(jnp.int32, (1, size), 1)
    per = 16 * rows
    source = (column % per) // rows * per + column // per * rows + column % rows
    return (lax.broadcasted_iota(jnp.int32, (size, size), 0) == source).astype(BF16)


def norm_kernel(xh_ref, own_ref, other_ref, gain_ref, shuffle_ref, out_ref):
    swapped = xh_ref[0] == 1
    for slot in range(2):
        here, there = (own_ref, other_ref) if slot == 0 else (other_ref, own_ref)
        x = jnp.where(swapped, there[...], here[...]).astype(F32)
        factor = lax.rsqrt(jnp.mean(x * x, axis=-1, keepdims=True) + EPSILON)
        normed = (x * factor * gain_ref[...]).astype(BF16)
        out_ref[:, slot] = dot(normed, shuffle_ref[...]).astype(BF16).reshape(8, 32, WIDTH)


def project_kernel(x_ref, w_ref, q_ref, kv_ref):
    step = pl.program_id(0)
    projected = dot(x_ref[...], w_ref[...].reshape(WIDTH, HALF)).astype(BF16)

    @pl.when(step == 0)
    def _():
        q_ref[...] = projected

    @pl.when(step > 0)
    def _():
        kv_ref[0] = projected


def attend(queries, keys, values, mask=None):
    outs = []
    for h, (first, last) in enumerate(((0, 128), (0, 256), (128, 384), (256, 384))):
        lane = lax.broadcasted_iota(jnp.int32, (1, last - first), 1) + first
        head = (lane >= h * HSIZE) & (lane < (h + 1) * HSIZE)
        q = jnp.where(head, queries[:, first:last], jnp.zeros((), BF16))
        scores = [dot_nt(q, k[:, first:last]) for k in keys]
        if mask is not None:
            scores = [jnp.where(mask, s, -jnp.inf) for s in scores]
        peak = functools.reduce(
            jnp.maximum, [jnp.max(s, axis=-1, keepdims=True) for s in scores]
        )
        terms = [jnp.exp2((s - peak) * SCALE) for s in scores]
        summed = sum(jnp.sum(t, axis=-1, keepdims=True) for t in terms)
        acc = sum(dot(t.astype(BF16), v[:, first:last]) for t, v in zip(terms, values))
        outs.append(acc * (1.0 / summed))
    lane = lax.broadcasted_iota(jnp.int32, (1, 128), 1)
    return (
        jnp.where(lane < 96, outs[0], outs[1][:, :128]),
        jnp.where(lane < 64, outs[1][:, 128:], outs[2][:, :128]),
        jnp.where(lane < 32, outs[2][:, 128:], outs[3]),
    )


def spatial_kernel(q_ref, kv_ref, kvo_ref, out_ref):
    blocks = attend(q_ref[...], (kv_ref[0], kvo_ref[0]), (kv_ref[1], kvo_ref[1]))
    for i, block in enumerate(blocks):
        out_ref[:, i * 128 : (i + 1) * 128] = block.astype(BF16)


def output_kernel(ctx_ref, tok_ref, w_ref, gain_ref, sh3_ref, sh6_ref, branch_ref, out_ref):
    rows = tok_ref.shape[0]
    ctx = jnp.concatenate(
        [ctx_ref[:, 0].reshape(rows, HALF), ctx_ref[:, 1].reshape(rows, HALF)], axis=1
    )
    ctx = dot(ctx, sh3_ref[...]).astype(BF16)
    mixed = []
    total = jnp.zeros((rows, 1), F32)
    for cb in range(4):
        lanes = slice(cb * HALF, (cb + 1) * HALF)
        w = w_ref[:, cb * 48 : (cb + 1) * 48, :].reshape(INNER, HALF)
        branch = dot(ctx, w).astype(BF16)
        branch_ref[:, lanes] = branch
        mix = tok_ref[:, lanes].astype(F32) + branch.astype(F32)
        mixed.append(mix)
        total += jnp.sum(mix * mix, axis=-1, keepdims=True)
    factor = lax.rsqrt(total * (1.0 / WIDTH) + EPSILON)
    target = lax.broadcasted_iota(jnp.int32, (rows, rows), 0)
    source = (target % 32) // 4 * 32 + target // 32 * 4 + target % 4
    swap = (lax.broadcasted_iota(jnp.int32, (rows, rows), 1) == source).astype(BF16)
    normed = jnp.concatenate(
        [
            (mix * factor * gain_ref[:, cb * HALF : (cb + 1) * HALF]).astype(BF16)
            for cb, mix in enumerate(mixed)
        ],
        axis=1,
    )
    normed = dot(swap, normed).astype(BF16)
    out_ref[...] = dot(normed, sh6_ref[...]).astype(BF16)


def temporal_kernel(x_ref, w_ref, out_ref):
    rows = x_ref.shape[0]
    query, key, value = (
        dot(x_ref[...], w_ref[:, 96 * i : 96 * (i + 1), :].reshape(WIDTH, HALF)).astype(BF16)
        for i in range(3)
    )
    r = lax.broadcasted_iota(jnp.int32, (rows, rows), 0)
    s = lax.broadcasted_iota(jnp.int32, (rows, rows), 1)
    same = (r % 4 == s % 4) & ((r // 8) % 2 == (s // 8) % 2)
    seen = (r // 16) * 2 + (r // 4) % 2 >= (s // 16) * 2 + (s // 4) % 2
    for i, block in enumerate(attend(query, (key,), (value,), same & seen)):
        out_ref[:, i * 128 : (i + 1) * 128] = block.astype(BF16)


def whole(shape):
    return pl.BlockSpec(shape, lambda *_: (0,) * len(shape))


def pick(first, a, b, axis):
    return jnp.where(first, jnp.concatenate([a, b], axis), jnp.concatenate([b, a], axis))


def per_device(tokens, space_gain, spatial_project, spatial_output, time_gain, temporal_project):
    core = lax.axis_index("core")
    x_hi = lax.axis_index("x_hi")
    tm = lax.axis_index(TM)
    swap = [(0, 1), (1, 0)]
    sh6 = shuffle(WIDTH, 6)
    sh3 = shuffle(INNER, 3)

    wq = lax.dynamic_slice_in_dim(spatial_project, tm * 6, 6, 0)
    wq = wq.reshape(6, 3, 2, HALF).transpose(2, 1, 0, 3).reshape(2, 18, HALF)
    wo = lax.dynamic_slice_in_dim(spatial_output, tm * 3, 3, 0)
    wo = wo.reshape(3, 4, HALF).transpose(1, 0, 2).reshape(12, HALF)
    wt = lax.dynamic_slice_in_dim(temporal_project, tm * 6, 6, 0)
    wt = wt.reshape(6, 3, 2, HALF).transpose(2, 1, 0, 3).reshape(36, HALF)
    chunk = jnp.stack([jnp.concatenate([wo, wq[i], wt], 0) for i in range(2)])
    chunk = jnp.broadcast_to(chunk[None], (8, 2, 66, HALF)).reshape(16, 66, HALF)
    got = lax.all_to_all(chunk, DP, 0, 0, tiled=True)
    across = lax.ppermute(tokens, "x_hi", swap)

    def both_cores(block):
        halves = block.reshape(4, 2, 32, WIDTH)
        keep = lax.dynamic_index_in_dim(halves, core, 1, keepdims=False)
        send = lax.dynamic_index_in_dim(halves, 1 - core, 1, keepdims=False)
        moved = lax.ppermute(send, "core", swap)
        return pick(core == 0, keep, moved, 0).reshape(256, WIDTH)

    frames = both_cores(tokens)
    normed = pl.pallas_call(
        norm_kernel,
        grid_spec=pltpu.PrefetchScalarGridSpec(
            num_scalar_prefetch=1,
            grid=(1,),
            in_specs=[
                whole((256, WIDTH)),
                whole((256, WIDTH)),
                whole((1, WIDTH)),
                whole((WIDTH, WIDTH)),
            ],
            out_specs=whole((8, 2, 32, WIDTH)),
        ),
        out_shape=jax.ShapeDtypeStruct((8, 2, 32, WIDTH), BF16),
        compiler_params=params(),
        name="space_norm",
    )(
        x_hi.reshape(1).astype(jnp.int32),
        frames,
        both_cores(across),
        space_gain.reshape(1, WIDTH),
        sh6,
    )
    got, _ = lax.optimization_barrier((got, normed))
    w1 = jnp.concatenate(
        [
            got[:, :12].reshape(16, 4, 3, HALF).transpose(1, 0, 2, 3).reshape(192, HALF),
            got[:, 12:30].reshape(16, 3, 6, HALF).transpose(1, 0, 2, 3).reshape(288, HALF),
        ],
        0,
    )
    w2 = got[:, 30:].reshape(16, 6, 6, HALF).transpose(1, 0, 2, 3).reshape(576, HALF)
    w1 = lax.all_gather(w1, TM, axis=0, tiled=False)
    frame = lax.all_to_all(normed.reshape(8, 64, WIDTH), "z", 0, 0, tiled=True)
    w2, frame = lax.optimization_barrier((w2, frame))
    w2 = lax.all_gather(w2, TM, axis=0, tiled=False)
    q, kv = pl.pallas_call(
        project_kernel,
        grid=(3,),
        in_specs=[
            whole((512, WIDTH)),
            pl.BlockSpec((16, 96, HALF), lambda i: (0, i + 2, 0)),
        ],
        out_specs=[
            whole((512, HALF)),
            pl.BlockSpec((1, 512, HALF), lambda i: (jnp.maximum(i - 1, 0), 0, 0)),
        ],
        out_shape=[
            jax.ShapeDtypeStruct((512, HALF), BF16),
            jax.ShapeDtypeStruct((2, 512, HALF), BF16),
        ],
        compiler_params=params(),
        name="space_project",
    )(frame.reshape(512, WIDTH), w1)
    kvo = lax.ppermute(kv, "core", swap)
    ctx = pl.pallas_call(
        spatial_kernel,
        grid=(2,),
        in_specs=[
            pl.BlockSpec((256, HALF), lambda i: (i, 0)),
            whole((2, 512, HALF)),
            whole((2, 512, HALF)),
        ],
        out_specs=pl.BlockSpec((256, HALF), lambda i: (i, 0)),
        out_shape=jax.ShapeDtypeStruct((512, HALF), BF16),
        compiler_params=params(),
        name="space_attend",
    )(q, kv, kvo)
    ctx = lax.all_to_all(ctx.reshape(16, 32, HALF), DP, 0, 0, tiled=True)
    branch, normed_time = pl.pallas_call(
        output_kernel,
        grid=(1,),
        in_specs=[
            whole((8, 2, 32, HALF)),
            whole((256, WIDTH)),
            whole((16, 192, HALF)),
            whole((1, WIDTH)),
            whole((INNER, INNER)),
            whole((WIDTH, WIDTH)),
        ],
        out_specs=[whole((256, WIDTH)), whole((256, WIDTH))],
        out_shape=[
            jax.ShapeDtypeStruct((256, WIDTH), BF16),
            jax.ShapeDtypeStruct((256, WIDTH), BF16),
        ],
        compiler_params=params(),
        name="space_output",
    )(ctx.reshape(8, 2, 32, HALF), frames, w1, time_gain.reshape(1, WIDTH), sh3, sh6)
    branch = branch.reshape(8, 32, WIDTH)
    mine = lax.dynamic_slice_in_dim(branch, core * 4, 4, 0)
    theirs = lax.dynamic_slice_in_dim(branch, (1 - core) * 4, 4, 0)
    back = lax.ppermute(theirs, "core", swap)
    branch = pick(core == 0, mine[:, None], back[:, None], 1).reshape(tokens.shape)

    columns = lax.all_to_all(normed_time.reshape(8, 32, WIDTH), TM[:2], 0, 0, tiled=True)
    context = pl.pallas_call(
        temporal_kernel,
        grid=(2,),
        in_specs=[
            whole((256, WIDTH)),
            pl.BlockSpec((16, 288, HALF), lambda i: (0, i, 0)),
        ],
        out_specs=pl.BlockSpec((256, HALF), lambda i: (0, i)),
        out_shape=jax.ShapeDtypeStruct((256, INNER), BF16),
        compiler_params=params(),
        name="time_attend",
    )(columns.reshape(256, WIDTH), w2)
    context = lax.all_to_all(context.reshape(16, 16, INNER), TM, 0, 0, tiled=True)
    context = context.reshape(8, 2, 2, 2, 4, INNER).transpose(2, 3, 1, 0, 4, 5)
    return branch, context.reshape(2, 2, 64, INNER)


def solution(mesh):
    fine = Mesh(mesh.devices.reshape(2, 4, 2, 8, 2), TM + DP)
    in_specs = (P(None, TM, DP, None), P(), P(DP, None), P(DP, None), P(), P(DP, None))
    out_specs = (P(None, TM, DP, None), P(None, TM, DP, None))
    return jax.shard_map(
        per_device, mesh=fine, in_specs=in_specs, out_specs=out_specs, check_vma=False
    )
```

```python
import functools
import math

import jax
import jax.numpy as jnp
import numpy as np
from jax import lax
from jax.experimental import pallas as pl
from jax.experimental.pallas import tpu as pltpu
from jax.sharding import Mesh
from jax.sharding import PartitionSpec as P

HEADS = 8
HSIZE = 96
WIDTH = 1536
INNER = 768
HALF = INNER // 2
EPSILON = 1e-05
SCALE = math.log2(math.e) / math.sqrt(HSIZE)
TM = ("x_lo", "y", "core")
DP = ("z", "x_hi")
BF16 = jnp.bfloat16
F32 = jnp.float32


def dot(a, b):
    return jnp.dot(a, b, preferred_element_type=F32)


def dot_nt(a, b):
    return lax.dot_general(a, b, (((1,), (1,)), ((), ())), preferred_element_type=F32)


def one_hot(shape, order):
    size = math.prod(shape)
    source = np.arange(size).reshape(shape).transpose(order).reshape(-1)
    return (np.arange(size)[:, None] == source[None]).astype(jnp.bfloat16)


def fetch(pairs, sems):
    copies = [pltpu.make_async_copy(a, b, sems.at[i]) for i, (a, b) in enumerate(pairs)]
    for copy in copies:
        copy.start()
    return copies


def gather_frames(core, block_ref, moved_ref, frames_vmem):
    frames_vmem[pl.ds(core * 4, 4)] = block_ref[:, pl.ds(core, 1)].reshape(4, 32, WIDTH)
    frames_vmem[pl.ds((1 - core) * 4, 4)] = moved_ref[...]


def normalize(frames_vmem, gain_ref):
    x = frames_vmem[...].reshape(256, WIDTH).astype(F32)
    factor = lax.rsqrt(jnp.mean(x * x, axis=-1, keepdims=True) + EPSILON)
    return (x * factor * gain_ref[...]).astype(BF16)


def own_kernel(
    core_ref, block_ref, moved_ref, gain_ref, order_ref,
    frames_ref, out_ref, frames_vmem, out_vmem, order_vmem, sems,
):
    copies = fetch([(order_ref, order_vmem)], sems)
    gather_frames(core_ref[0], block_ref, moved_ref, frames_vmem)
    copies += fetch([(frames_vmem, frames_ref)], sems.at[pl.ds(1, 1)])
    normed = normalize(frames_vmem, gain_ref)
    copies[0].wait()
    out_vmem[...] = dot(normed, order_vmem[...]).astype(BF16).reshape(8, 1, 32, WIDTH)
    copies += fetch([(out_vmem, out_ref)], sems.at[pl.ds(2, 1)])
    copies[1].wait()
    copies[2].wait()


def other_kernel(
    core_ref, xh_ref, block_ref, moved_ref, gain_ref, own_ref, order_ref,
    out_ref, frames_vmem, own_vmem, order_vmem, sems,
):
    copies = fetch([(order_ref, order_vmem), (own_ref, own_vmem)], sems)
    xh = xh_ref[0]
    gather_frames(core_ref[0], block_ref, moved_ref, frames_vmem)
    normed = normalize(frames_vmem, gain_ref)
    copies[0].wait()
    other = dot(normed, order_vmem[...]).astype(BF16)
    out_ref[:, pl.ds(1 - xh, 1)] = other.reshape(8, 1, 32, WIDTH)
    copies[1].wait()
    out_ref[:, pl.ds(xh, 1)] = own_vmem[...]


def project_kernel(x_ref, w_ref, q_ref, kv_ref, w_vmem, sems):
    copies = fetch(
        [(w_ref.at[:, pl.ds(192 + 96 * i, 96)], w_vmem.at[i]) for i in range(3)], sems
    )
    for copy, i in zip(copies, range(3)):
        copy.wait()
        projected = dot(x_ref[...], w_vmem[i].reshape(WIDTH, HALF)).astype(BF16)
        if i == 0:
            q_ref[...] = projected
        else:
            kv_ref[i - 1] = projected


def attend(queries, keys, values, mask=None):
    outs = []
    for h, (first, last) in enumerate(((0, 128), (0, 256), (128, 384), (256, 384))):
        lane = lax.broadcasted_iota(jnp.int32, (1, last - first), 1) + first
        head = (lane >= h * HSIZE) & (lane < (h + 1) * HSIZE)
        q = jnp.where(head, queries[:, first:last], jnp.zeros((), BF16))
        scores = [dot_nt(q, k[:, first:last]) for k in keys]
        if mask is not None:
            scores = [jnp.where(mask, s, -jnp.inf) for s in scores]
        peak = functools.reduce(
            jnp.maximum, [jnp.max(s, axis=-1, keepdims=True) for s in scores]
        )
        terms = [jnp.exp2((s - peak) * SCALE) for s in scores]
        summed = sum(jnp.sum(t, axis=-1, keepdims=True) for t in terms)
        acc = sum(dot(t.astype(BF16), v[:, first:last]) for t, v in zip(terms, values))
        outs.append(acc * (1.0 / summed))
    lane = lax.broadcasted_iota(jnp.int32, (1, 128), 1)
    return (
        jnp.where(lane < 96, outs[0], outs[1][:, :128]),
        jnp.where(lane < 64, outs[1][:, 128:], outs[2][:, :128]),
        jnp.where(lane < 32, outs[2][:, 128:], outs[3]),
    )


def spatial_kernel(q_ref, kv_ref, kvo_ref, out_ref):
    for first in (0, 256):
        rows = slice(first, first + 256)
        blocks = attend(q_ref[rows], (kv_ref[0], kvo_ref[0]), (kv_ref[1], kvo_ref[1]))
        for i, block in enumerate(blocks):
            out_ref[rows, i * 128 : (i + 1) * 128] = block.astype(BF16)


def weights_kernel(
    w_ref, inner_ref, time_ref,
    plain_ref, mixed_ref, w_vmem, inner_vmem, time_vmem, plain_vmem, mixed_vmem, sems,
):
    copies = fetch(
        [
            (inner_ref, inner_vmem),
            (w_ref.at[:, pl.ds(0, 192)], w_vmem),
            (time_ref, time_vmem),
        ],
        sems,
    )
    copies[0].wait()
    copies[1].wait()
    for cb in range(4):
        w = w_vmem[:, cb * 48 : (cb + 1) * 48, :].reshape(INNER, HALF)
        plain_vmem[:, cb * HALF : (cb + 1) * HALF] = dot(inner_vmem[...], w).astype(BF16)
    copies[2].wait()
    out = fetch([(plain_vmem, plain_ref)], sems.at[pl.ds(3, 1)])
    for cb in range(4):
        lanes = slice(cb * HALF, (cb + 1) * HALF)
        mixed_vmem[cb] = dot(plain_vmem[...], time_vmem[:, lanes]).astype(BF16)
        out += fetch([(mixed_vmem.at[cb], mixed_ref.at[cb])], sems.at[pl.ds(4 + cb, 1)])
    for copy in out:
        copy.wait()


def tokens_kernel(tok_ref, time_ref, out_ref, tok_vmem, time_vmem, out_vmem, sems):
    for copy in fetch([(tok_ref, tok_vmem), (time_ref, time_vmem)], sems):
        copy.wait()
    out_vmem[...] = dot(tok_vmem[...], time_vmem[...]).astype(BF16)
    fetch([(out_vmem, out_ref)], sems.at[pl.ds(2, 1)])[0].wait()


def join(ctx_ref):
    rows = 256
    return jnp.concatenate(
        [ctx_ref[:, 0].reshape(rows, HALF), ctx_ref[:, 1].reshape(rows, HALF)], axis=1
    )


def output_kernel(ctx_ref, tok_ref, w_ref, gain_ref, out_ref, w_vmem, tok_vmem, sems):
    copies = fetch(
        [(w_ref.at[cb], w_vmem.at[cb]) for cb in range(4)] + [(tok_ref, tok_vmem)], sems
    )
    rows = tok_ref.shape[0]
    ctx = join(ctx_ref)
    target = lax.broadcasted_iota(jnp.int32, (rows, rows), 0)
    source = (target % 32) // 4 * 32 + target // 32 * 4 + target % 4
    swap = (lax.broadcasted_iota(jnp.int32, (rows, rows), 1) == source).astype(BF16)
    branches = []
    for cb in range(4):
        copies[cb].wait()
        branches.append(dot(ctx, w_vmem[cb]).astype(BF16))
    copies[4].wait()
    mixed = []
    total = jnp.zeros((rows, 1), F32)
    for cb, branch in enumerate(branches):
        mix = tok_vmem[:, cb * HALF : (cb + 1) * HALF].astype(F32) + branch.astype(F32)
        mixed.append(mix)
        total += jnp.sum(mix * mix, axis=-1, keepdims=True)
    factor = lax.rsqrt(total * (1.0 / WIDTH) + EPSILON)
    for cb, mix in enumerate(mixed):
        lanes = slice(cb * HALF, (cb + 1) * HALF)
        normed = (mix * factor * gain_ref[:, lanes]).astype(BF16)
        out_ref[:, lanes] = dot(swap, normed).astype(BF16)


def branch_kernel(ctx_ref, w_ref, out_ref, w_vmem, sems):
    copies = fetch([(w_ref, w_vmem)], sems)
    ctx = join(ctx_ref)
    copies[0].wait()
    for cb in range(4):
        lanes = slice(cb * HALF, (cb + 1) * HALF)
        out_ref[:, lanes] = dot(ctx, w_vmem[:, lanes]).astype(BF16)


def temporal_kernel(x_ref, w_ref, out_ref, w_vmem, sems):
    copies = fetch([(w_ref.at[:, pl.ds(96 * i, 96)], w_vmem.at[i]) for i in range(6)], sems)
    rows = x_ref.shape[0]
    r = lax.broadcasted_iota(jnp.int32, (rows, rows), 0)
    s = lax.broadcasted_iota(jnp.int32, (rows, rows), 1)
    same = (r % 4 == s % 4) & ((r // 8) % 2 == (s // 8) % 2)
    seen = (r // 16) * 2 + (r // 4) % 2 >= (s // 16) * 2 + (s // 4) % 2
    for half in range(2):
        parts = []
        for i in range(3 * half, 3 * half + 3):
            copies[i].wait()
            parts.append(dot(x_ref[...], w_vmem[i].reshape(WIDTH, HALF)).astype(BF16))
        query, key, value = parts
        for i, block in enumerate(attend(query, (key,), (value,), same & seen)):
            lanes = slice(half * HALF + i * 128, half * HALF + (i + 1) * 128)
            out_ref[:, lanes] = block.astype(BF16)


SMEM = pl.BlockSpec(memory_space=pltpu.SMEM)
VMEM = pl.BlockSpec(memory_space=pltpu.VMEM)
HBM = pl.BlockSpec(memory_space=pltpu.HBM)


def call(kernel, name, specs, out_shapes, scratch, copies, mib=32, cost=None):
    if copies:
        scratch = scratch + [pltpu.SemaphoreType.DMA((copies,))]
    return pl.pallas_call(
        kernel,
        in_specs=specs,
        out_specs=[pl.BlockSpec(memory_space=space) for space, _ in out_shapes],
        out_shape=[
            pltpu.HBM(shape, BF16) if space is pltpu.HBM else jax.ShapeDtypeStruct(shape, BF16)
            for space, shape in out_shapes
        ],
        scratch_shapes=scratch,
        compiler_params=pltpu.CompilerParams(vmem_limit_bytes=mib * 1024 * 1024),
        cost_estimate=cost,
        name=name,
    )


def hbm(x):
    return pltpu.with_memory_space_constraint(x, pltpu.HBM)


def vmem(*shape):
    return pltpu.VMEM(shape, BF16)


def pick(first, a, b, axis):
    return jnp.where(first, jnp.concatenate([a, b], axis), jnp.concatenate([b, a], axis))


def per_device(tokens, space_gain, spatial_project, spatial_output, time_gain, temporal_project):
    core = lax.axis_index("core")
    x_hi = lax.axis_index("x_hi")
    tm = lax.axis_index(TM)
    swap = [(0, 1), (1, 0)]
    space_order = jnp.asarray(one_hot((16, 16, 6), (1, 0, 2)))
    inner_order = jnp.asarray(one_hot((16, 16, 3), (1, 0, 2)))
    time_order = jnp.asarray(one_hot((16, 16, 2, 3), (1, 2, 0, 3)))

    wq = lax.dynamic_slice_in_dim(spatial_project, tm * 6, 6, 0)
    wq = wq.reshape(6, 3, 2, HALF).transpose(2, 1, 0, 3).reshape(2, 18, HALF)
    wo = lax.dynamic_slice_in_dim(spatial_output, tm * 3, 3, 0)
    wo = wo.reshape(3, 4, HALF).transpose(1, 0, 2).reshape(12, HALF)
    wt = lax.dynamic_slice_in_dim(temporal_project, tm * 6, 6, 0)
    wt = wt.reshape(2, 3, 3, 2, HALF).transpose(0, 3, 2, 1, 4).reshape(2, 18, HALF)
    chunk = jnp.stack([jnp.concatenate([wo, wq[i], wt[i]], 0) for i in range(2)])
    chunk = jnp.broadcast_to(chunk[None], (8, 2, 48, HALF)).reshape(16, 48, HALF)
    got = lax.all_to_all(chunk, DP, 0, 0, tiled=True)
    across = lax.ppermute(tokens, "x_hi", swap)

    def moved(block):
        return lax.ppermute(
            lax.dynamic_index_in_dim(block, 1 - core, 1, keepdims=False), "core", swap
        )

    core_id = core.reshape(1).astype(jnp.int32)
    xh_id = x_hi.reshape(1).astype(jnp.int32)
    gain = space_gain.reshape(1, WIDTH)
    halves = tokens.reshape(4, 2, 32, WIDTH)
    frames, own = call(
        own_kernel,
        "space_norm_own",
        [SMEM] + [VMEM] * 3 + [HBM],
        [(pltpu.HBM, (8, 32, WIDTH)), (pltpu.HBM, (8, 1, 32, WIDTH))],
        [vmem(8, 32, WIDTH), vmem(8, 1, 32, WIDTH), vmem(WIDTH, WIDTH)],
        3,
        20,
        cost=pl.CostEstimate(flops=1, bytes_accessed=1, transcendentals=0),
    )(core_id, halves, moved(halves), gain, hbm(space_order))
    across, own = lax.optimization_barrier((across, own))
    halves = across.reshape(4, 2, 32, WIDTH)
    (normed,) = call(
        other_kernel,
        "space_norm_other",
        [SMEM] * 2 + [VMEM] * 3 + [HBM] * 2,
        [(pltpu.VMEM, (8, 2, 32, WIDTH))],
        [vmem(8, 32, WIDTH), vmem(8, 1, 32, WIDTH), vmem(WIDTH, WIDTH)],
        2,
        20,
    )(core_id, xh_id, halves, moved(halves), gain, hbm(own), hbm(space_order))
    got, normed = lax.optimization_barrier((got, normed))
    w1 = jnp.concatenate(
        [
            got[:, :12].reshape(16, 4, 3, HALF).transpose(1, 0, 2, 3).reshape(192, HALF),
            got[:, 12:30].reshape(16, 3, 6, HALF).transpose(1, 0, 2, 3).reshape(288, HALF),
        ],
        0,
    )
    w2 = got[:, 30:].reshape(16, 6, 3, HALF).transpose(1, 0, 2, 3).reshape(6, 1, 48, HALF)
    w2 = pick(x_hi == 0, w2, lax.ppermute(w2, "x_hi", swap), 1).reshape(576, HALF)
    w1 = lax.all_gather(w1, TM, axis=0, tiled=False)
    (tokens_time,) = call(
        tokens_kernel,
        "time_tokens",
        [HBM] * 2,
        [(pltpu.HBM, (256, WIDTH))],
        [vmem(256, WIDTH), vmem(WIDTH, WIDTH), vmem(256, WIDTH)],
        3,
        16,
    )(hbm(frames.reshape(256, WIDTH)), hbm(time_order))
    frame = lax.all_to_all(normed.reshape(8, 64, WIDTH), "z", 0, 0, tiled=True)
    w2, frame, tokens_time = lax.optimization_barrier((w2, frame, tokens_time))
    w2 = lax.all_gather(w2, TM, axis=0, tiled=False)
    q, kv = call(
        project_kernel,
        "space_project",
        [VMEM, HBM],
        [(pltpu.VMEM, (512, HALF)), (pltpu.VMEM, (2, 512, HALF))],
        [vmem(3, 16, 96, HALF)],
        3,
    )(frame.reshape(512, WIDTH), hbm(w1))
    kvo = lax.ppermute(kv, "core", swap)
    (ctx,) = call(spatial_kernel, "space_attend", [VMEM] * 3, [(pltpu.VMEM, (512, HALF))], [], 0, 20)(
        q, kv, kvo
    )
    w1, ctx = lax.optimization_barrier((w1, ctx))
    plain, mixed = call(
        weights_kernel,
        "output_weights",
        [HBM] * 3,
        [(pltpu.HBM, (INNER, WIDTH)), (pltpu.HBM, (4, INNER, HALF))],
        [
            vmem(16, 192, HALF),
            vmem(INNER, INNER),
            vmem(WIDTH, WIDTH),
            vmem(INNER, WIDTH),
            vmem(4, INNER, HALF),
        ],
        8,
        24,
        cost=pl.CostEstimate(flops=5_400_000_000, bytes_accessed=15_000_000, transcendentals=0),
    )(hbm(w1), hbm(inner_order), hbm(time_order))
    gain = time_gain.reshape(16, 16, 2, 3).transpose(1, 2, 0, 3).reshape(1, WIDTH)
    ctx = lax.all_to_all(ctx.reshape(16, 32, HALF), DP, 0, 0, tiled=True).reshape(8, 2, 32, HALF)
    (normed_time,) = call(
        output_kernel,
        "space_output",
        [VMEM, HBM, HBM, VMEM],
        [(pltpu.VMEM, (256, WIDTH))],
        [vmem(4, INNER, HALF), vmem(256, WIDTH)],
        5,
        20,
    )(ctx, hbm(tokens_time), hbm(mixed), gain)
    ctx, normed_time = lax.optimization_barrier((ctx, normed_time))
    (branch,) = call(
        branch_kernel,
        "space_branch",
        [VMEM, HBM],
        [(pltpu.VMEM, (256, WIDTH))],
        [vmem(INNER, WIDTH)],
        1,
        12,
    )(ctx, hbm(plain))
    branch = branch.reshape(8, 32, WIDTH)
    mine = lax.dynamic_slice_in_dim(branch, core * 4, 4, 0)
    theirs = lax.dynamic_slice_in_dim(branch, (1 - core) * 4, 4, 0)
    back = lax.ppermute(theirs, "core", swap)
    branch = pick(core == 0, mine[:, None], back[:, None], 1).reshape(tokens.shape)

    columns = lax.all_to_all(normed_time.reshape(8, 32, WIDTH), TM[:2], 0, 0, tiled=True)
    (context,) = call(
        temporal_kernel,
        "time_attend",
        [VMEM, HBM],
        [(pltpu.VMEM, (256, INNER))],
        [vmem(6, 16, 96, HALF)],
        6,
    )(columns.reshape(256, WIDTH), hbm(w2))
    context = lax.all_to_all(context.reshape(16, 16, INNER), TM, 0, 0, tiled=True)
    context = context.reshape(8, 2, 2, 2, 4, INNER).transpose(2, 3, 1, 0, 4, 5)
    return branch, context.reshape(2, 2, 64, INNER)


def solution(mesh):
    fine = Mesh(mesh.devices.reshape(2, 4, 2, 8, 2), TM + DP)
    in_specs = (P(None, TM, DP, None), P(), P(DP, None), P(DP, None), P(), P(DP, None))
    out_specs = (P(None, TM, DP, None), P(None, TM, DP, None))
    return jax.shard_map(
        per_device, mesh=fine, in_specs=in_specs, out_specs=out_specs, check_vma=False
    )
```

```python
import functools
import math

import jax
import jax.numpy as jnp
import numpy as np
from jax import lax
from jax.experimental import pallas as pl
from jax.experimental.pallas import tpu as pltpu
from jax.sharding import Mesh
from jax.sharding import PartitionSpec as P

HEADS = 8
HSIZE = 96
WIDTH = 1536
INNER = 768
HALF = INNER // 2
EPSILON = 1e-05
SCALE = math.log2(math.e) / math.sqrt(HSIZE)
TM = ("x_lo", "y", "core")
DP = ("z", "x_hi")
BF16 = jnp.bfloat16
F32 = jnp.float32


def dot(a, b):
    return jnp.dot(a, b, preferred_element_type=F32)


def dot_nt(a, b):
    return lax.dot_general(a, b, (((1,), (1,)), ((), ())), preferred_element_type=F32)


def one_hot(shape, order):
    size = math.prod(shape)
    source = np.arange(size).reshape(shape).transpose(order).reshape(-1)
    return (np.arange(size)[:, None] == source[None]).astype(jnp.bfloat16)


def fetch(pairs, sems):
    copies = [pltpu.make_async_copy(a, b, sems.at[i]) for i, (a, b) in enumerate(pairs)]
    for copy in copies:
        copy.start()
    return copies


def gather_frames(core, block_ref, moved_ref, frames_vmem):
    frames_vmem[pl.ds(core * 4, 4)] = block_ref[:, pl.ds(core, 1)].reshape(4, 32, WIDTH)
    frames_vmem[pl.ds((1 - core) * 4, 4)] = moved_ref[...]


def normalize(frames_vmem, gain_ref):
    x = frames_vmem[...].reshape(256, WIDTH).astype(F32)
    factor = lax.rsqrt(jnp.mean(x * x, axis=-1, keepdims=True) + EPSILON)
    return (x * factor * gain_ref[...]).astype(BF16)


def own_kernel(
    core_ref, block_ref, moved_ref, gain_ref, order_ref,
    frames_ref, out_ref, frames_vmem, out_vmem, order_vmem, sems,
):
    copies = fetch([(order_ref, order_vmem)], sems)
    gather_frames(core_ref[0], block_ref, moved_ref, frames_vmem)
    copies += fetch([(frames_vmem, frames_ref)], sems.at[pl.ds(1, 1)])
    normed = normalize(frames_vmem, gain_ref)
    copies[0].wait()
    out_vmem[...] = dot(normed, order_vmem[...]).astype(BF16).reshape(8, 1, 32, WIDTH)
    copies += fetch([(out_vmem, out_ref)], sems.at[pl.ds(2, 1)])
    copies[1].wait()
    copies[2].wait()


def other_kernel(
    core_ref, xh_ref, block_ref, moved_ref, gain_ref, own_ref, order_ref,
    out_ref, frames_vmem, own_vmem, order_vmem, sems,
):
    copies = fetch([(order_ref, order_vmem), (own_ref, own_vmem)], sems)
    xh = xh_ref[0]
    gather_frames(core_ref[0], block_ref, moved_ref, frames_vmem)
    normed = normalize(frames_vmem, gain_ref)
    copies[0].wait()
    other = dot(normed, order_vmem[...]).astype(BF16)
    out_ref[:, pl.ds(1 - xh, 1)] = other.reshape(8, 1, 32, WIDTH)
    copies[1].wait()
    out_ref[:, pl.ds(xh, 1)] = own_vmem[...]


def project_kernel(x_ref, w_ref, q_ref, kv_ref, w_vmem, sems):
    copies = fetch(
        [(w_ref.at[:, pl.ds(192 + 96 * i, 96)], w_vmem.at[i]) for i in range(3)], sems
    )
    for copy, i in zip(copies, range(3)):
        copy.wait()
        projected = dot(x_ref[...], w_vmem[i].reshape(WIDTH, HALF)).astype(BF16)
        if i == 0:
            q_ref[...] = projected
        else:
            kv_ref[i - 1] = projected


def attend(queries, keys, values, mask=None):
    outs = []
    for h, (first, last) in enumerate(((0, 128), (0, 256), (128, 384), (256, 384))):
        lane = lax.broadcasted_iota(jnp.int32, (1, last - first), 1) + first
        head = (lane >= h * HSIZE) & (lane < (h + 1) * HSIZE)
        q = jnp.where(head, queries[:, first:last], jnp.zeros((), BF16))
        scores = [dot_nt(q, k[:, first:last]) for k in keys]
        if mask is not None:
            scores = [jnp.where(mask, s, -jnp.inf) for s in scores]
        peak = functools.reduce(
            jnp.maximum, [jnp.max(s, axis=-1, keepdims=True) for s in scores]
        )
        terms = [jnp.exp2((s - peak) * SCALE) for s in scores]
        summed = sum(jnp.sum(t, axis=-1, keepdims=True) for t in terms)
        acc = sum(dot(t.astype(BF16), v[:, first:last]) for t, v in zip(terms, values))
        outs.append(acc * (1.0 / summed))
    lane = lax.broadcasted_iota(jnp.int32, (1, 128), 1)
    return (
        jnp.where(lane < 96, outs[0], outs[1][:, :128]),
        jnp.where(lane < 64, outs[1][:, 128:], outs[2][:, :128]),
        jnp.where(lane < 32, outs[2][:, 128:], outs[3]),
    )


def spatial_kernel(q_ref, kv_ref, kvo_ref, out_ref):
    for first in (0, 256):
        rows = slice(first, first + 256)
        blocks = attend(q_ref[rows], (kv_ref[0], kvo_ref[0]), (kv_ref[1], kvo_ref[1]))
        for i, block in enumerate(blocks):
            block = block.astype(BF16).reshape(4, 2, 32, 128)
            for xh in range(2):
                z = slice(first // 64, first // 64 + 4)
                out_ref[xh, z, :, i * 128 : (i + 1) * 128] = block[:, xh]


def weights_kernel(
    w_ref, inner_ref, time_ref,
    plain_ref, mixed_ref, w_vmem, inner_vmem, time_vmem, plain_vmem, mixed_vmem, sems,
):
    copies = fetch(
        [
            (inner_ref, inner_vmem),
            (w_ref.at[:, pl.ds(0, 192)], w_vmem),
            (time_ref, time_vmem),
        ],
        sems,
    )
    copies[0].wait()
    copies[1].wait()
    for cb in range(4):
        w = w_vmem[:, cb * 48 : (cb + 1) * 48, :].reshape(INNER, HALF)
        plain_vmem[:, cb * HALF : (cb + 1) * HALF] = dot(inner_vmem[...], w).astype(BF16)
    copies[2].wait()
    out = fetch([(plain_vmem, plain_ref)], sems.at[pl.ds(3, 1)])
    for cb in range(4):
        lanes = slice(cb * HALF, (cb + 1) * HALF)
        mixed_vmem[cb] = dot(plain_vmem[...], time_vmem[:, lanes]).astype(BF16)
        out += fetch([(mixed_vmem.at[cb], mixed_ref.at[cb])], sems.at[pl.ds(4 + cb, 1)])
    for copy in out:
        copy.wait()


def tokens_kernel(tok_ref, time_ref, out_ref, tok_vmem, time_vmem, out_vmem, sems):
    for copy in fetch([(tok_ref, tok_vmem), (time_ref, time_vmem)], sems):
        copy.wait()
    out_vmem[...] = dot(tok_vmem[...], time_vmem[...]).astype(BF16)
    fetch([(out_vmem, out_ref)], sems.at[pl.ds(2, 1)])[0].wait()


def output_kernel(ctx_ref, tok_ref, w_ref, gain_ref, out_ref, w_vmem, tok_vmem, sems):
    copies = fetch(
        [(w_ref.at[cb], w_vmem.at[cb]) for cb in range(4)] + [(tok_ref, tok_vmem)], sems
    )
    rows = tok_ref.shape[0]
    ctx = jnp.concatenate([ctx_ref[0], ctx_ref[1]], axis=1)
    target = lax.broadcasted_iota(jnp.int32, (rows, rows), 0)
    source = (target % 64) // 8 * 32 + target // 64 * 8 + target % 8
    swap = (lax.broadcasted_iota(jnp.int32, (rows, rows), 1) == source).astype(BF16)
    branches = []
    for cb in range(4):
        copies[cb].wait()
        branches.append(dot(ctx, w_vmem[cb]).astype(BF16))
    copies[4].wait()
    mixed = []
    total = jnp.zeros((rows, 1), F32)
    for cb, branch in enumerate(branches):
        mix = tok_vmem[:, cb * HALF : (cb + 1) * HALF].astype(F32) + branch.astype(F32)
        mixed.append(mix)
        total += jnp.sum(mix * mix, axis=-1, keepdims=True)
    factor = lax.rsqrt(total * (1.0 / WIDTH) + EPSILON)
    for cb, mix in enumerate(mixed):
        lanes = slice(cb * HALF, (cb + 1) * HALF)
        normed = (mix * factor * gain_ref[:, lanes]).astype(BF16)
        normed = dot(swap, normed).astype(BF16)
        out_ref[0, :, lanes] = normed
        out_ref[1, :, lanes] = normed


def branch_kernel(ctx_ref, w_ref, out_ref, w_vmem, sems):
    copies = fetch([(w_ref, w_vmem)], sems)
    ctx = jnp.concatenate([ctx_ref[0], ctx_ref[1]], axis=1)
    copies[0].wait()
    for cb in range(4):
        lanes = slice(cb * HALF, (cb + 1) * HALF)
        out_ref[:, lanes] = dot(ctx, w_vmem[:, lanes]).astype(BF16)


def temporal_kernel(x_ref, w_ref, out_ref, w_vmem, sems):
    copies = fetch([(w_ref.at[:, pl.ds(192 * i, 192)], w_vmem.at[i]) for i in range(3)], sems)
    r = lax.broadcasted_iota(jnp.int32, (256, 256), 0)
    s = lax.broadcasted_iota(jnp.int32, (256, 256), 1)
    mask = (r % 8 == s % 8) & (r // 8 >= s // 8)
    parts = []
    for i in range(3):
        copies[i].wait()
        part = dot(x_ref[...], w_vmem[i].reshape(WIDTH, HALF)).astype(BF16)
        parts.append(part.reshape(16, 2, 16, HALF))
    for history in range(2):
        query, key, value = (part[:, history].reshape(256, HALF) for part in parts)
        for i, block in enumerate(attend(query, (key,), (value,), mask)):
            block = block.astype(BF16).reshape(16, 16, 128)
            out_ref[:, history, :, i * 128 : (i + 1) * 128] = block


SMEM = pl.BlockSpec(memory_space=pltpu.SMEM)
VMEM = pl.BlockSpec(memory_space=pltpu.VMEM)
HBM = pl.BlockSpec(memory_space=pltpu.HBM)


def call(kernel, name, specs, out_shapes, scratch, copies, mib=32, cost=None):
    if copies:
        scratch = scratch + [pltpu.SemaphoreType.DMA((copies,))]
    return pl.pallas_call(
        kernel,
        in_specs=specs,
        out_specs=[pl.BlockSpec(memory_space=space) for space, _ in out_shapes],
        out_shape=[
            pltpu.HBM(shape, BF16) if space is pltpu.HBM else jax.ShapeDtypeStruct(shape, BF16)
            for space, shape in out_shapes
        ],
        scratch_shapes=scratch,
        compiler_params=pltpu.CompilerParams(vmem_limit_bytes=mib * 1024 * 1024),
        cost_estimate=cost,
        name=name,
    )


def hbm(x):
    return pltpu.with_memory_space_constraint(x, pltpu.HBM)


def vmem(*shape):
    return pltpu.VMEM(shape, BF16)


def pick(first, a, b, axis):
    return jnp.where(first, jnp.concatenate([a, b], axis), jnp.concatenate([b, a], axis))


def per_device(tokens, space_gain, spatial_project, spatial_output, time_gain, temporal_project):
    core = lax.axis_index("core")
    x_lo = lax.axis_index("x_lo")
    x_hi = lax.axis_index("x_hi")
    tm = lax.axis_index(TM)
    swap = [(0, 1), (1, 0)]
    space_order = jnp.asarray(one_hot((16, 16, 6), (1, 0, 2)))
    inner_order = jnp.asarray(one_hot((16, 16, 3), (1, 0, 2)))
    time_order = jnp.asarray(one_hot((16, 4, 2, 2, 6), (1, 2, 3, 0, 4)))

    wq = lax.dynamic_slice_in_dim(spatial_project, tm * 6, 6, 0)
    wq = wq.reshape(6, 3, 2, HALF).transpose(2, 1, 0, 3).reshape(2, 18, HALF)
    wo = lax.dynamic_slice_in_dim(spatial_output, tm * 3, 3, 0)
    wo = wo.reshape(3, 4, HALF).transpose(1, 0, 2).reshape(12, HALF)
    row = lax.axis_index(TM[1:]) * 12
    wt = lax.dynamic_slice_in_dim(temporal_project, row, 12, 0).reshape(2, 6, 3, 2, HALF)
    wt = lax.dynamic_index_in_dim(wt, x_lo, 3, keepdims=False)
    wt = wt.transpose(0, 2, 1, 3).reshape(2, 18, HALF)
    chunk = jnp.stack([jnp.concatenate([wo, wq[i], wt[i]], 0) for i in range(2)])
    chunk = jnp.broadcast_to(chunk[None], (8, 2, 48, HALF)).reshape(16, 48, HALF)
    got = lax.all_to_all(chunk, DP, 0, 0, tiled=True)
    across = lax.ppermute(tokens, "x_hi", swap)

    def moved(block):
        return lax.ppermute(
            lax.dynamic_index_in_dim(block, 1 - core, 1, keepdims=False), "core", swap
        )

    core_id = core.reshape(1).astype(jnp.int32)
    xh_id = x_hi.reshape(1).astype(jnp.int32)
    gain = space_gain.reshape(1, WIDTH)
    halves = tokens.reshape(4, 2, 32, WIDTH)
    frames, own = call(
        own_kernel,
        "space_norm_own",
        [SMEM] + [VMEM] * 3 + [HBM],
        [(pltpu.HBM, (8, 32, WIDTH)), (pltpu.HBM, (8, 1, 32, WIDTH))],
        [vmem(8, 32, WIDTH), vmem(8, 1, 32, WIDTH), vmem(WIDTH, WIDTH)],
        3,
        20,
        cost=pl.CostEstimate(flops=1, bytes_accessed=1, transcendentals=0),
    )(core_id, halves, moved(halves), gain, hbm(space_order))
    across, own = lax.optimization_barrier((across, own))
    halves = across.reshape(4, 2, 32, WIDTH)
    (normed,) = call(
        other_kernel,
        "space_norm_other",
        [SMEM] * 2 + [VMEM] * 3 + [HBM] * 2,
        [(pltpu.VMEM, (8, 2, 32, WIDTH))],
        [vmem(8, 32, WIDTH), vmem(8, 1, 32, WIDTH), vmem(WIDTH, WIDTH)],
        2,
        20,
    )(core_id, xh_id, halves, moved(halves), gain, hbm(own), hbm(space_order))
    got, normed = lax.optimization_barrier((got, normed))
    w1 = jnp.concatenate(
        [
            got[:, :12].reshape(16, 4, 3, HALF).transpose(1, 0, 2, 3).reshape(192, HALF),
            got[:, 12:30].reshape(16, 3, 6, HALF).transpose(1, 0, 2, 3).reshape(288, HALF),
        ],
        0,
    )
    w2 = got[:, 30:].reshape(16, 3, 6, HALF).transpose(1, 0, 2, 3).reshape(3, 1, 96, HALF)
    w2 = pick(x_hi == 0, w2, lax.ppermute(w2, "x_hi", swap), 1).reshape(576, HALF)
    w1 = lax.all_gather(w1, TM, axis=0, tiled=False)
    (tokens_time,) = call(
        tokens_kernel,
        "time_tokens",
        [HBM] * 2,
        [(pltpu.HBM, (256, WIDTH))],
        [vmem(256, WIDTH), vmem(WIDTH, WIDTH), vmem(256, WIDTH)],
        3,
        16,
    )(hbm(frames.reshape(256, WIDTH)), hbm(time_order))
    frame = lax.all_to_all(normed.reshape(8, 64, WIDTH), "z", 0, 0, tiled=True)
    w2, frame, tokens_time = lax.optimization_barrier((w2, frame, tokens_time))
    w2 = lax.all_gather(w2, TM[1:], axis=0, tiled=False)
    q, kv = call(
        project_kernel,
        "space_project",
        [VMEM, HBM],
        [(pltpu.VMEM, (512, HALF)), (pltpu.VMEM, (2, 512, HALF))],
        [vmem(3, 16, 96, HALF)],
        3,
    )(frame.reshape(512, WIDTH), hbm(w1))
    kvo = lax.ppermute(kv, "core", swap)
    (ctx,) = call(spatial_kernel, "space_attend", [VMEM] * 3, [(pltpu.VMEM, (2, 8, 32, HALF))], [], 0, 20)(
        q, kv, kvo
    )
    w1, ctx = lax.optimization_barrier((w1, ctx))
    plain, mixed = call(
        weights_kernel,
        "output_weights",
        [HBM] * 3,
        [(pltpu.HBM, (INNER, WIDTH)), (pltpu.HBM, (4, INNER, HALF))],
        [
            vmem(16, 192, HALF),
            vmem(INNER, INNER),
            vmem(WIDTH, WIDTH),
            vmem(INNER, WIDTH),
            vmem(4, INNER, HALF),
        ],
        8,
        24,
        cost=pl.CostEstimate(flops=5_400_000_000, bytes_accessed=15_000_000, transcendentals=0),
    )(hbm(w1), hbm(inner_order), hbm(time_order))
    gain = time_gain.reshape(16, 4, 2, 2, 6).transpose(1, 2, 3, 0, 4).reshape(1, WIDTH)
    ctx = lax.all_to_all(ctx.reshape(16, 32, HALF), DP[::-1], 0, 0, tiled=True)
    ctx = ctx.reshape(2, 256, HALF)
    (normed_time,) = call(
        output_kernel,
        "space_output",
        [VMEM, HBM, HBM, VMEM],
        [(pltpu.VMEM, (2, 256, WIDTH))],
        [vmem(4, INNER, HALF), vmem(256, WIDTH)],
        5,
        20,
    )(ctx, hbm(tokens_time), hbm(mixed), gain)
    ctx, normed_time = lax.optimization_barrier((ctx, normed_time))
    (branch,) = call(
        branch_kernel,
        "space_branch",
        [VMEM, HBM],
        [(pltpu.VMEM, (256, WIDTH))],
        [vmem(INNER, WIDTH)],
        1,
        12,
    )(ctx, hbm(plain))
    branch = branch.reshape(8, 32, WIDTH)
    mine = lax.dynamic_slice_in_dim(branch, core * 4, 4, 0)
    theirs = lax.dynamic_slice_in_dim(branch, (1 - core) * 4, 4, 0)
    back = lax.ppermute(theirs, "core", swap)
    branch = pick(core == 0, mine[:, None], back[:, None], 1).reshape(tokens.shape)

    columns = lax.all_to_all(normed_time.reshape(8, 64, WIDTH), TM[:2], 0, 0, tiled=True)
    (context,) = call(
        temporal_kernel,
        "time_attend",
        [VMEM, HBM],
        [(pltpu.VMEM, (16, 2, 16, HALF))],
        [vmem(3, 8, 192, HALF)],
        3,
    )(columns.reshape(512, WIDTH), hbm(w2))
    context = lax.all_to_all(context.reshape(16, 32, HALF), TM, 0, 0, tiled=True)
    context = context.reshape(2, 4, 2, 2, 2, 8, HALF).transpose(3, 4, 2, 1, 5, 0, 6)
    return branch, context.reshape(2, 2, 64, INNER)


def solution(mesh):
    fine = Mesh(mesh.devices.reshape(2, 4, 2, 8, 2), TM + DP)
    in_specs = (P(None, TM, DP, None), P(), P(DP, None), P(DP, None), P(), P(DP, None))
    out_specs = (P(None, TM, DP, None), P(None, TM, DP, None))
    return jax.shard_map(
        per_device, mesh=fine, in_specs=in_specs, out_specs=out_specs, check_vma=False
    )
```

```python
import functools
import math

import jax
import jax.numpy as jnp
import numpy as np
from jax import lax
from jax.experimental import pallas as pl
from jax.experimental.pallas import tpu as pltpu
from jax.sharding import Mesh
from jax.sharding import PartitionSpec as P

HEADS = 8
HSIZE = 96
WIDTH = 1536
INNER = 768
HALF = INNER // 2
EPSILON = 1e-05
SCALE = math.log2(math.e) / math.sqrt(HSIZE)
TM = ("x_lo", "y", "core")
DP = ("z", "x_hi")
BF16 = jnp.bfloat16
F32 = jnp.float32


def dot(a, b):
    return jnp.dot(a, b, preferred_element_type=F32)


def dot_nt(a, b):
    return lax.dot_general(a, b, (((1,), (1,)), ((), ())), preferred_element_type=F32)


def one_hot(shape, order):
    size = math.prod(shape)
    source = np.arange(size).reshape(shape).transpose(order).reshape(-1)
    return (np.arange(size)[:, None] == source[None]).astype(jnp.bfloat16)


def fetch(pairs, sems):
    copies = [pltpu.make_async_copy(a, b, sems.at[i]) for i, (a, b) in enumerate(pairs)]
    for copy in copies:
        copy.start()
    return copies


def chunk_kernel(tm_ref, wq_ref, wo_ref, wt_ref, out_ref):
    tm = tm_ref[0]
    half = pl.multiple_of(tm // 8 * HALF, HALF)
    for h in range(2):
        pieces = [(wo_ref[:, cb * HALF : (cb + 1) * HALF], 3 * cb, 3, tm * 3) for cb in range(4)]
        for kind in range(3):
            first = kind * INNER + h * HALF
            pieces.append((wq_ref[:, first : first + HALF], 12 + 6 * kind, 6, tm * 6))
            lanes = pl.ds(pl.multiple_of(kind * INNER + half, HALF), HALF)
            pieces.append((wt_ref[:, lanes], 30 + 6 * kind, 6, tm % 8 * 12 + h * 6))
        total = jnp.zeros((48, HALF), F32)
        for block, place, count, source in pieces:
            row = lax.broadcasted_iota(jnp.int32, (48, block.shape[0]), 0) - place
            column = lax.broadcasted_iota(jnp.int32, (48, block.shape[0]), 1) - source
            picked = (row == column) & (row >= 0) & (row < count)
            total += dot(picked.astype(BF16), block)
        for z in range(8):
            out_ref[z, h] = total.astype(BF16)


def gather_frames(core, block_ref, moved_ref, frames_vmem):
    frames_vmem[pl.ds(core * 4, 4)] = block_ref[:, pl.ds(core, 1)].reshape(4, 32, WIDTH)
    frames_vmem[pl.ds((1 - core) * 4, 4)] = moved_ref[...]


def normalize(frames_vmem, gain_ref):
    x = frames_vmem[...].reshape(256, WIDTH).astype(F32)
    factor = lax.rsqrt(jnp.mean(x * x, axis=-1, keepdims=True) + EPSILON)
    return (x * factor * gain_ref[...]).astype(BF16)


def own_kernel(
    core_ref, block_ref, moved_ref, gain_ref, order_ref,
    frames_ref, out_ref, frames_vmem, out_vmem, order_vmem, sems,
):
    copies = fetch([(order_ref, order_vmem)], sems)
    gather_frames(core_ref[0], block_ref, moved_ref, frames_vmem)
    copies += fetch([(frames_vmem, frames_ref)], sems.at[pl.ds(1, 1)])
    normed = normalize(frames_vmem, gain_ref)
    copies[0].wait()
    out_vmem[...] = dot(normed, order_vmem[...]).astype(BF16).reshape(8, 1, 32, WIDTH)
    copies += fetch([(out_vmem, out_ref)], sems.at[pl.ds(2, 1)])
    copies[1].wait()
    copies[2].wait()


def other_kernel(
    core_ref, xh_ref, block_ref, moved_ref, gain_ref, own_ref, order_ref,
    out_ref, frames_vmem, order_vmem, sems,
):
    xh = xh_ref[0]
    pairs = [
        (order_ref.at[:, pl.ds(cb * HALF, HALF)], order_vmem.at[cb]) for cb in range(4)
    ]
    copies = fetch(pairs + [(own_ref, out_ref.at[:, pl.ds(xh, 1)])], sems)
    gather_frames(core_ref[0], block_ref, moved_ref, frames_vmem)
    normed = normalize(frames_vmem, gain_ref)
    for cb in range(4):
        copies[cb].wait()
        other = dot(normed, order_vmem[cb]).astype(BF16).reshape(8, 1, 32, HALF)
        out_ref[:, pl.ds(1 - xh, 1), :, cb * HALF : (cb + 1) * HALF] = other
    copies[4].wait()


def keys_values_kernel(x_ref, w_ref, kv_ref, w_vmem, sems):
    copies = fetch(
        [(w_ref.at[:, pl.ds(192 + 96 * i, 96)], w_vmem.at[i - 1]) for i in (1, 2)], sems
    )
    for i in range(2):
        copies[i].wait()
        kv_ref[i] = dot(x_ref[...], w_vmem[i].reshape(WIDTH, HALF)).astype(BF16)


def queries_kernel(x_ref, w_ref, q_ref, w_vmem, sems):
    fetch([(w_ref.at[:, pl.ds(192, 96)], w_vmem)], sems)[0].wait()
    q_ref[...] = dot(x_ref[...], w_vmem[...].reshape(WIDTH, HALF)).astype(BF16)


def attend(queries, keys, values, mask=None):
    outs = []
    for h, (first, last) in enumerate(((0, 128), (0, 256), (128, 384), (256, 384))):
        lane = lax.broadcasted_iota(jnp.int32, (1, last - first), 1) + first
        head = (lane >= h * HSIZE) & (lane < (h + 1) * HSIZE)
        q = jnp.where(head, queries[:, first:last], jnp.zeros((), BF16))
        scores = [dot_nt(q, k[:, first:last]) for k in keys]
        if mask is not None:
            scores = [jnp.where(mask, s, -jnp.inf) for s in scores]
        peak = functools.reduce(
            jnp.maximum, [jnp.max(s, axis=-1, keepdims=True) for s in scores]
        )
        terms = [jnp.exp2((s - peak) * SCALE) for s in scores]
        summed = sum(jnp.sum(t, axis=-1, keepdims=True) for t in terms)
        acc = sum(dot(t.astype(BF16), v[:, first:last]) for t, v in zip(terms, values))
        outs.append(acc * (1.0 / summed))
    lane = lax.broadcasted_iota(jnp.int32, (1, 128), 1)
    return (
        jnp.where(lane < 96, outs[0], outs[1][:, :128]),
        jnp.where(lane < 64, outs[1][:, 128:], outs[2][:, :128]),
        jnp.where(lane < 32, outs[2][:, 128:], outs[3]),
    )


def spatial_kernel(q_ref, kv_ref, kvo_ref, out_ref):
    for first in (0, 256):
        rows = slice(first, first + 256)
        blocks = attend(q_ref[rows], (kv_ref[0], kvo_ref[0]), (kv_ref[1], kvo_ref[1]))
        for i, block in enumerate(blocks):
            block = block.astype(BF16).reshape(4, 2, 32, 128)
            for xh in range(2):
                z = slice(first // 64, first // 64 + 4)
                out_ref[xh, z, :, i * 128 : (i + 1) * 128] = block[:, xh]


def weights_kernel(
    w_ref, inner_ref, time_ref,
    plain_ref, mixed_ref, w_vmem, inner_vmem, time_vmem, plain_vmem, mixed_vmem, sems,
):
    copies = fetch(
        [
            (inner_ref, inner_vmem),
            (w_ref.at[:, pl.ds(0, 192)], w_vmem),
            (time_ref, time_vmem),
        ],
        sems,
    )
    copies[0].wait()
    copies[1].wait()
    for cb in range(4):
        w = w_vmem[:, cb * 48 : (cb + 1) * 48, :].reshape(INNER, HALF)
        plain_vmem[:, cb * HALF : (cb + 1) * HALF] = dot(inner_vmem[...], w).astype(BF16)
    copies[2].wait()
    out = fetch([(plain_vmem, plain_ref)], sems.at[pl.ds(3, 1)])
    for cb in range(4):
        lanes = slice(cb * HALF, (cb + 1) * HALF)
        mixed_vmem[cb] = dot(plain_vmem[...], time_vmem[:, lanes]).astype(BF16)
        out += fetch([(mixed_vmem.at[cb], mixed_ref.at[cb])], sems.at[pl.ds(4 + cb, 1)])
    for copy in out:
        copy.wait()


def tokens_kernel(tok_ref, time_ref, out_ref, tok_vmem, time_vmem, out_vmem, sems):
    for copy in fetch([(tok_ref, tok_vmem), (time_ref, time_vmem)], sems):
        copy.wait()
    out_vmem[...] = dot(tok_vmem[...], time_vmem[...]).astype(BF16)
    fetch([(out_vmem, out_ref)], sems.at[pl.ds(2, 1)])[0].wait()


def output_kernel(
    ctx_ref, tok_ref, w_ref, gain_ref, out_ref, w_vmem, tok_vmem, out_vmem, sems
):
    copies = fetch(
        [(w_ref.at[cb], w_vmem.at[cb]) for cb in range(4)] + [(tok_ref, tok_vmem)], sems
    )
    rows = tok_ref.shape[0]
    ctx = jnp.concatenate([ctx_ref[0], ctx_ref[1]], axis=1)
    target = lax.broadcasted_iota(jnp.int32, (rows, rows), 0)
    source = (target % 64) // 8 * 32 + target // 64 * 8 + target % 8
    swap = (lax.broadcasted_iota(jnp.int32, (rows, rows), 1) == source).astype(BF16)
    branches = []
    for cb in range(4):
        copies[cb].wait()
        branches.append(dot(ctx, w_vmem[cb]).astype(BF16))
    copies[4].wait()
    mixed = []
    total = jnp.zeros((rows, 1), F32)
    for cb, branch in enumerate(branches):
        mix = tok_vmem[:, cb * HALF : (cb + 1) * HALF].astype(F32) + branch.astype(F32)
        mixed.append(mix)
        total += jnp.sum(mix * mix, axis=-1, keepdims=True)
    factor = lax.rsqrt(total * (1.0 / WIDTH) + EPSILON)
    for cb, mix in enumerate(mixed):
        lanes = slice(cb * HALF, (cb + 1) * HALF)
        normed = (mix * factor * gain_ref[:, lanes]).astype(BF16)
        out_vmem[cb] = dot(swap, normed).astype(BF16)
        for i in range(2):
            place = out_ref.at[i, :, pl.ds(cb * HALF, HALF)]
            copies += fetch([(out_vmem.at[cb], place)], sems.at[pl.ds(5 + 2 * cb + i, 1)])
    for copy in copies[5:]:
        copy.wait()


def branch_kernel(ctx_ref, w_ref, out_ref, w_vmem, sems):
    copies = fetch([(w_ref, w_vmem)], sems)
    ctx = jnp.concatenate([ctx_ref[0], ctx_ref[1]], axis=1)
    copies[0].wait()
    for cb in range(4):
        lanes = slice(cb * HALF, (cb + 1) * HALF)
        out_ref[:, lanes] = dot(ctx, w_vmem[:, lanes]).astype(BF16)


def temporal_kernel(x_ref, w_ref, out_ref, w_vmem, sems):
    copies = fetch([(w_ref.at[:, pl.ds(192 * i, 192)], w_vmem.at[i]) for i in range(3)], sems)
    r = lax.broadcasted_iota(jnp.int32, (256, 256), 0)
    s = lax.broadcasted_iota(jnp.int32, (256, 256), 1)
    mask = (r % 8 == s % 8) & (r // 8 >= s // 8)
    parts = []
    for i in range(3):
        copies[i].wait()
        part = dot(x_ref[...], w_vmem[i].reshape(WIDTH, HALF)).astype(BF16)
        parts.append(part.reshape(16, 2, 16, HALF))
    for history in range(2):
        query, key, value = (part[:, history].reshape(256, HALF) for part in parts)
        for i, block in enumerate(attend(query, (key,), (value,), mask)):
            block = block.astype(BF16).reshape(16, 16, 128)
            out_ref[:, history, :, i * 128 : (i + 1) * 128] = block


SMEM = pl.BlockSpec(memory_space=pltpu.SMEM)
VMEM = pl.BlockSpec(memory_space=pltpu.VMEM)
HBM = pl.BlockSpec(memory_space=pltpu.HBM)


def call(kernel, name, specs, out_shapes, scratch, copies, mib=32, cost=None):
    if copies:
        scratch = scratch + [pltpu.SemaphoreType.DMA((copies,))]
    return pl.pallas_call(
        kernel,
        in_specs=specs,
        out_specs=[pl.BlockSpec(memory_space=space) for space, _ in out_shapes],
        out_shape=[
            pltpu.HBM(shape, BF16) if space is pltpu.HBM else jax.ShapeDtypeStruct(shape, BF16)
            for space, shape in out_shapes
        ],
        scratch_shapes=scratch,
        compiler_params=pltpu.CompilerParams(vmem_limit_bytes=mib * 1024 * 1024),
        cost_estimate=cost,
        name=name,
    )


def hbm(x):
    return pltpu.with_memory_space_constraint(x, pltpu.HBM)


def vmem(*shape):
    return pltpu.VMEM(shape, BF16)


def pick(first, a, b, axis):
    return jnp.where(first, jnp.concatenate([a, b], axis), jnp.concatenate([b, a], axis))


def per_device(tokens, space_gain, spatial_project, spatial_output, time_gain, temporal_project):
    core = lax.axis_index("core")
    x_lo = lax.axis_index("x_lo")
    x_hi = lax.axis_index("x_hi")
    tm = lax.axis_index(TM)
    swap = [(0, 1), (1, 0)]
    space_order = jnp.asarray(one_hot((16, 16, 6), (1, 0, 2)))
    inner_order = jnp.asarray(one_hot((16, 16, 3), (1, 0, 2)))
    time_order = jnp.asarray(one_hot((16, 4, 2, 2, 6), (1, 2, 3, 0, 4)))

    (chunk,) = call(
        chunk_kernel,
        "weight_rows",
        [SMEM] + [VMEM] * 3,
        [(pltpu.VMEM, (8, 2, 48, HALF))],
        [],
        0,
        12,
    )(tm.reshape(1).astype(jnp.int32), spatial_project, spatial_output, temporal_project)
    chunk = chunk.reshape(16, 48, HALF)
    got = lax.all_to_all(chunk, DP, 0, 0, tiled=True)
    across = lax.ppermute(tokens, "x_hi", swap)

    def moved(block):
        return lax.ppermute(
            lax.dynamic_index_in_dim(block, 1 - core, 1, keepdims=False), "core", swap
        )

    core_id = core.reshape(1).astype(jnp.int32)
    xh_id = x_hi.reshape(1).astype(jnp.int32)
    gain = space_gain.reshape(1, WIDTH)
    halves = tokens.reshape(4, 2, 32, WIDTH)
    frames, own = call(
        own_kernel,
        "space_norm_own",
        [SMEM] + [VMEM] * 3 + [HBM],
        [(pltpu.HBM, (8, 32, WIDTH)), (pltpu.HBM, (8, 1, 32, WIDTH))],
        [vmem(8, 32, WIDTH), vmem(8, 1, 32, WIDTH), vmem(WIDTH, WIDTH)],
        3,
        20,
        cost=pl.CostEstimate(flops=1, bytes_accessed=1, transcendentals=0),
    )(core_id, halves, moved(halves), gain, hbm(space_order))
    across, own = lax.optimization_barrier((across, own))
    halves = across.reshape(4, 2, 32, WIDTH)
    (normed,) = call(
        other_kernel,
        "space_norm_other",
        [SMEM] * 2 + [VMEM] * 3 + [HBM] * 2,
        [(pltpu.VMEM, (8, 2, 32, WIDTH))],
        [vmem(8, 32, WIDTH), vmem(4, WIDTH, HALF)],
        5,
        20,
    )(core_id, xh_id, halves, moved(halves), gain, hbm(own), hbm(space_order))
    got, normed = lax.optimization_barrier((got, normed))
    w1 = jnp.concatenate(
        [
            got[:, :12].reshape(16, 4, 3, HALF).transpose(1, 0, 2, 3).reshape(192, HALF),
            got[:, 12:30].reshape(16, 3, 6, HALF).transpose(1, 0, 2, 3).reshape(288, HALF),
        ],
        0,
    )
    w2 = got[:, 30:].reshape(16, 3, 6, HALF).transpose(1, 0, 2, 3).reshape(3, 1, 96, HALF)
    w2 = pick(x_hi == 0, w2, lax.ppermute(w2, "x_hi", swap), 1).reshape(576, HALF)
    w1 = lax.all_gather(w1, TM, axis=0, tiled=False)
    (tokens_time,) = call(
        tokens_kernel,
        "time_tokens",
        [HBM] * 2,
        [(pltpu.HBM, (256, WIDTH))],
        [vmem(256, WIDTH), vmem(WIDTH, WIDTH), vmem(256, WIDTH)],
        3,
        16,
    )(hbm(frames.reshape(256, WIDTH)), hbm(time_order))
    frame = lax.all_to_all(normed.reshape(8, 64, WIDTH), "z", 0, 0, tiled=True)
    w2, frame, tokens_time = lax.optimization_barrier((w2, frame, tokens_time))
    w2 = lax.all_gather(w2, TM[1:], axis=0, tiled=False)
    frame = frame.reshape(512, WIDTH)
    (kv,) = call(
        keys_values_kernel,
        "space_keys_values",
        [VMEM, HBM],
        [(pltpu.VMEM, (2, 512, HALF))],
        [vmem(2, 16, 96, HALF)],
        2,
        24,
    )(frame, hbm(w1))
    kvo = lax.ppermute(kv, "core", swap)
    frame, kv = lax.optimization_barrier((frame, kv))
    (q,) = call(
        queries_kernel,
        "space_queries",
        [VMEM, HBM],
        [(pltpu.VMEM, (512, HALF))],
        [vmem(16, 96, HALF)],
        1,
        16,
    )(frame, hbm(w1))
    (ctx,) = call(spatial_kernel, "space_attend", [VMEM] * 3, [(pltpu.VMEM, (2, 8, 32, HALF))], [], 0, 20)(
        q, kv, kvo
    )
    w1, ctx = lax.optimization_barrier((w1, ctx))
    plain, mixed = call(
        weights_kernel,
        "output_weights",
        [HBM] * 3,
        [(pltpu.HBM, (INNER, WIDTH)), (pltpu.HBM, (4, INNER, HALF))],
        [
            vmem(16, 192, HALF),
            vmem(INNER, INNER),
            vmem(WIDTH, WIDTH),
            vmem(INNER, WIDTH),
            vmem(4, INNER, HALF),
        ],
        8,
        24,
        cost=pl.CostEstimate(flops=5_400_000_000, bytes_accessed=15_000_000, transcendentals=0),
    )(hbm(w1), hbm(inner_order), hbm(time_order))
    gain = time_gain.reshape(16, 4, 2, 2, 6).transpose(1, 2, 3, 0, 4).reshape(1, WIDTH)
    ctx = lax.all_to_all(ctx.reshape(16, 32, HALF), DP[::-1], 0, 0, tiled=True)
    ctx = ctx.reshape(2, 256, HALF)
    (normed_time,) = call(
        output_kernel,
        "space_output",
        [VMEM, HBM, HBM, VMEM],
        [(pltpu.HBM, (2, 256, WIDTH))],
        [vmem(4, INNER, HALF), vmem(256, WIDTH), vmem(4, 256, HALF)],
        13,
        20,
    )(ctx, hbm(tokens_time), hbm(mixed), gain)
    ctx, normed_time = lax.optimization_barrier((ctx, normed_time))
    (branch,) = call(
        branch_kernel,
        "space_branch",
        [VMEM, HBM],
        [(pltpu.VMEM, (256, WIDTH))],
        [vmem(INNER, WIDTH)],
        1,
        12,
    )(ctx, hbm(plain))
    branch = branch.reshape(8, 32, WIDTH)
    mine = lax.dynamic_slice_in_dim(branch, core * 4, 4, 0)
    theirs = lax.dynamic_slice_in_dim(branch, (1 - core) * 4, 4, 0)
    back = lax.ppermute(theirs, "core", swap)
    branch = pick(core == 0, mine[:, None], back[:, None], 1).reshape(tokens.shape)

    columns = lax.all_to_all(normed_time.reshape(8, 64, WIDTH), TM[:2], 0, 0, tiled=True)
    (context,) = call(
        temporal_kernel,
        "time_attend",
        [VMEM, HBM],
        [(pltpu.VMEM, (16, 2, 16, HALF))],
        [vmem(3, 8, 192, HALF)],
        3,
    )(columns.reshape(512, WIDTH), hbm(w2))
    context = lax.all_to_all(context.reshape(16, 32, HALF), TM, 0, 0, tiled=True)
    context = context.reshape(2, 4, 2, 2, 2, 8, HALF).transpose(3, 4, 2, 1, 5, 0, 6)
    return branch, context.reshape(2, 2, 64, INNER)


def solution(mesh):
    fine = Mesh(mesh.devices.reshape(2, 4, 2, 8, 2), TM + DP)
    in_specs = (P(None, TM, DP, None), P(), P(DP, None), P(DP, None), P(), P(DP, None))
    out_specs = (P(None, TM, DP, None), P(None, TM, DP, None))
    return jax.shard_map(
        per_device, mesh=fine, in_specs=in_specs, out_specs=out_specs, check_vma=False
    )
```

```python
import functools
import math

import jax
import jax.numpy as jnp
import numpy as np
from jax import lax
from jax.experimental import pallas as pl
from jax.experimental.pallas import tpu as pltpu
from jax.sharding import Mesh
from jax.sharding import PartitionSpec as P

HEADS = 8
HSIZE = 96
WIDTH = 1536
INNER = 768
HALF = INNER // 2
EPSILON = 1e-05
SCALE = math.log2(math.e) / math.sqrt(HSIZE)
TM = ("x_lo", "y", "core")
DP = ("z", "x_hi")
PLANES = (0, 4, 2, 6, 1, 5, 3, 7)
BF16 = jnp.bfloat16
F32 = jnp.float32


def dot(a, b):
    return jnp.dot(a, b, preferred_element_type=F32)


def dot_nt(a, b):
    return lax.dot_general(a, b, (((1,), (1,)), ((), ())), preferred_element_type=F32)


def one_hot(shape, order):
    size = math.prod(shape)
    source = np.arange(size).reshape(shape).transpose(order).reshape(-1)
    return (np.arange(size)[:, None] == source[None]).astype(jnp.bfloat16)


def fetch(pairs, sems):
    copies = [pltpu.make_async_copy(a, b, sems.at[i]) for i, (a, b) in enumerate(pairs)]
    for copy in copies:
        copy.start()
    return copies


def chunk_kernel(tm_ref, wq_ref, wo_ref, wt_ref, out_ref):
    tm = tm_ref[0]
    half = pl.multiple_of(tm // 8 * HALF, HALF)
    for h in range(2):
        pieces = [(wo_ref[:, cb * HALF : (cb + 1) * HALF], 3 * cb, 3, tm * 3) for cb in range(4)]
        for kind in range(3):
            first = kind * INNER + h * HALF
            pieces.append((wq_ref[:, first : first + HALF], 12 + 6 * kind, 6, tm * 6))
            lanes = pl.ds(pl.multiple_of(kind * INNER + half, HALF), HALF)
            pieces.append((wt_ref[:, lanes], 30 + 6 * kind, 6, tm % 8 * 12 + h * 6))
        total = jnp.zeros((48, HALF), F32)
        for block, place, count, source in pieces:
            row = lax.broadcasted_iota(jnp.int32, (48, block.shape[0]), 0) - place
            column = lax.broadcasted_iota(jnp.int32, (48, block.shape[0]), 1) - source
            picked = (row == column) & (row >= 0) & (row < count)
            total += dot(picked.astype(BF16), block)
        for z in range(8):
            out_ref[z, h] = total.astype(BF16)


def gather_frames(core, block_ref, moved_ref, frames_vmem):
    frames_vmem[pl.ds(core * 4, 4)] = block_ref[:, pl.ds(core, 1)].reshape(4, 32, WIDTH)
    frames_vmem[pl.ds((1 - core) * 4, 4)] = moved_ref[...]


def normalize(frames_vmem, gain_ref):
    x = frames_vmem[...].reshape(256, WIDTH).astype(F32)
    factor = lax.rsqrt(jnp.mean(x * x, axis=-1, keepdims=True) + EPSILON)
    return (x * factor * gain_ref[...]).astype(BF16)


def own_kernel(
    core_ref, block_ref, moved_ref, gain_ref, order_ref,
    frames_ref, out_ref, frames_vmem, out_vmem, order_vmem, sems,
):
    copies = fetch([(order_ref, order_vmem)], sems)
    gather_frames(core_ref[0], block_ref, moved_ref, frames_vmem)
    copies += fetch([(frames_vmem, frames_ref)], sems.at[pl.ds(1, 1)])
    normed = normalize(frames_vmem, gain_ref)
    copies[0].wait()
    out_vmem[...] = dot(normed, order_vmem[...]).astype(BF16).reshape(8, 1, 32, WIDTH)
    copies += fetch([(out_vmem, out_ref)], sems.at[pl.ds(2, 1)])
    copies[1].wait()
    copies[2].wait()


def other_kernel(
    core_ref, xh_ref, block_ref, moved_ref, gain_ref, own_ref, order_ref,
    out_ref, frames_vmem, order_vmem, sems,
):
    xh = xh_ref[0]
    pairs = [
        (order_ref.at[:, pl.ds(cb * HALF, HALF)], order_vmem.at[cb]) for cb in range(4)
    ]
    copies = fetch(pairs + [(own_ref, out_ref.at[:, pl.ds(xh, 1)])], sems)
    gather_frames(core_ref[0], block_ref, moved_ref, frames_vmem)
    normed = normalize(frames_vmem, gain_ref)
    for cb in range(4):
        copies[cb].wait()
        other = dot(normed, order_vmem[cb]).astype(BF16).reshape(8, 1, 32, HALF)
        out_ref[:, pl.ds(1 - xh, 1), :, cb * HALF : (cb + 1) * HALF] = other
    copies[4].wait()


def keys_values_kernel(x_ref, w_ref, kv_ref, w_vmem, sems):
    copies = fetch(
        [(w_ref.at[:, pl.ds(192 + 96 * i, 96)], w_vmem.at[i - 1]) for i in (1, 2)], sems
    )
    for i in range(2):
        copies[i].wait()
        kv_ref[i] = dot(x_ref[...], w_vmem[i].reshape(WIDTH, HALF)).astype(BF16)


def queries_kernel(x_ref, w_ref, q_ref, w_vmem, sems):
    fetch([(w_ref.at[:, pl.ds(192, 96)], w_vmem)], sems)[0].wait()
    q_ref[...] = dot(x_ref[...], w_vmem[...].reshape(WIDTH, HALF)).astype(BF16)


def attend(queries, keys, values, mask=None):
    outs = []
    for h, (first, last) in enumerate(((0, 128), (0, 256), (128, 384), (256, 384))):
        lane = lax.broadcasted_iota(jnp.int32, (1, last - first), 1) + first
        head = (lane >= h * HSIZE) & (lane < (h + 1) * HSIZE)
        q = jnp.where(head, queries[:, first:last], jnp.zeros((), BF16))
        scores = [dot_nt(q, k[:, first:last]) for k in keys]
        if mask is not None:
            scores = [jnp.where(mask, s, -jnp.inf) for s in scores]
        peak = functools.reduce(
            jnp.maximum, [jnp.max(s, axis=-1, keepdims=True) for s in scores]
        )
        terms = [jnp.exp2((s - peak) * SCALE) for s in scores]
        summed = sum(jnp.sum(t, axis=-1, keepdims=True) for t in terms)
        acc = sum(dot(t.astype(BF16), v[:, first:last]) for t, v in zip(terms, values))
        outs.append(acc * (1.0 / summed))
    lane = lax.broadcasted_iota(jnp.int32, (1, 128), 1)
    return (
        jnp.where(lane < 96, outs[0], outs[1][:, :128]),
        jnp.where(lane < 64, outs[1][:, 128:], outs[2][:, :128]),
        jnp.where(lane < 32, outs[2][:, 128:], outs[3]),
    )


def spatial_kernel(q_ref, kv_ref, kvo_ref, out_ref):
    for first in (0, 256):
        rows = slice(first, first + 256)
        blocks = attend(q_ref[rows], (kv_ref[0], kvo_ref[0]), (kv_ref[1], kvo_ref[1]))
        for i, block in enumerate(blocks):
            block = block.astype(BF16).reshape(4, 2, 32, 128)
            for k in range(4):
                z = PLANES[first // 64 + k]
                for xh in range(2):
                    out_ref[xh, z, :, i * 128 : (i + 1) * 128] = block[k, xh]


def weights_kernel(
    w_ref, inner_ref, time_ref,
    plain_ref, mixed_ref, w_vmem, inner_vmem, time_vmem, plain_vmem, mixed_vmem, sems,
):
    copies = fetch(
        [
            (inner_ref, inner_vmem),
            (w_ref.at[:, pl.ds(0, 192)], w_vmem),
            (time_ref, time_vmem),
        ],
        sems,
    )
    copies[0].wait()
    copies[1].wait()
    for cb in range(4):
        w = w_vmem[:, cb * 48 : (cb + 1) * 48, :].reshape(INNER, HALF)
        plain_vmem[:, cb * HALF : (cb + 1) * HALF] = dot(inner_vmem[...], w).astype(BF16)
    copies[2].wait()
    out = fetch([(plain_vmem, plain_ref)], sems.at[pl.ds(3, 1)])
    for cb in range(4):
        lanes = slice(cb * HALF, (cb + 1) * HALF)
        mixed_vmem[cb] = dot(plain_vmem[...], time_vmem[:, lanes]).astype(BF16)
        out += fetch([(mixed_vmem.at[cb], mixed_ref.at[cb])], sems.at[pl.ds(4 + cb, 1)])
    for copy in out:
        copy.wait()


def tokens_kernel(tok_ref, time_ref, out_ref, tok_vmem, time_vmem, out_vmem, sems):
    for copy in fetch([(tok_ref, tok_vmem), (time_ref, time_vmem)], sems):
        copy.wait()
    out_vmem[...] = dot(tok_vmem[...], time_vmem[...]).astype(BF16)
    fetch([(out_vmem, out_ref)], sems.at[pl.ds(2, 1)])[0].wait()


def join(ctx_ref):
    rows = [
        jnp.concatenate([ctx_ref[i, 32 * z : 32 * z + 32] for z in PLANES], axis=0)
        for i in range(2)
    ]
    return jnp.concatenate(rows, axis=1)


def output_kernel(
    ctx_ref, tok_ref, w_ref, gain_ref, out_ref, w_vmem, tok_vmem, out_vmem, sems
):
    copies = fetch(
        [(w_ref.at[cb], w_vmem.at[cb]) for cb in range(4)] + [(tok_ref, tok_vmem)], sems
    )
    rows = tok_ref.shape[0]
    ctx = join(ctx_ref)
    target = lax.broadcasted_iota(jnp.int32, (rows, rows), 0)
    source = (target % 64) // 8 * 32 + target // 64 * 8 + target % 8
    swap = (lax.broadcasted_iota(jnp.int32, (rows, rows), 1) == source).astype(BF16)
    branches = []
    for cb in range(4):
        copies[cb].wait()
        branches.append(dot(ctx, w_vmem[cb]).astype(BF16))
    copies[4].wait()
    mixed = []
    total = jnp.zeros((rows, 1), F32)
    for cb, branch in enumerate(branches):
        mix = tok_vmem[:, cb * HALF : (cb + 1) * HALF].astype(F32) + branch.astype(F32)
        mixed.append(mix)
        total += jnp.sum(mix * mix, axis=-1, keepdims=True)
    factor = lax.rsqrt(total * (1.0 / WIDTH) + EPSILON)
    for cb, mix in enumerate(mixed):
        lanes = slice(cb * HALF, (cb + 1) * HALF)
        normed = (mix * factor * gain_ref[:, lanes]).astype(BF16)
        out_vmem[cb] = dot(swap, normed).astype(BF16)
        for i in range(2):
            place = out_ref.at[i, :, pl.ds(cb * HALF, HALF)]
            copies += fetch([(out_vmem.at[cb], place)], sems.at[pl.ds(5 + 2 * cb + i, 1)])
    for copy in copies[5:]:
        copy.wait()


def branch_kernel(ctx_ref, w_ref, out_ref, w_vmem, sems):
    copies = fetch([(w_ref, w_vmem)], sems)
    ctx = join(ctx_ref)
    copies[0].wait()
    for cb in range(4):
        lanes = slice(cb * HALF, (cb + 1) * HALF)
        out_ref[:, lanes] = dot(ctx, w_vmem[:, lanes]).astype(BF16)


def temporal_kernel(x_ref, w_ref, out_ref, w_vmem, sems):
    copies = fetch([(w_ref.at[:, pl.ds(192 * i, 192)], w_vmem.at[i]) for i in range(3)], sems)
    r = lax.broadcasted_iota(jnp.int32, (256, 256), 0)
    s = lax.broadcasted_iota(jnp.int32, (256, 256), 1)
    mask = (r % 8 == s % 8) & (r // 8 >= s // 8)
    parts = []
    for i in range(3):
        copies[i].wait()
        part = dot(x_ref[...], w_vmem[i].reshape(WIDTH, HALF)).astype(BF16)
        parts.append(part.reshape(16, 2, 16, HALF))
    for history in range(2):
        query, key, value = (part[:, history].reshape(256, HALF) for part in parts)
        for i, block in enumerate(attend(query, (key,), (value,), mask)):
            block = block.astype(BF16).reshape(16, 16, 128)
            out_ref[:, history, :, i * 128 : (i + 1) * 128] = block


SMEM = pl.BlockSpec(memory_space=pltpu.SMEM)
VMEM = pl.BlockSpec(memory_space=pltpu.VMEM)
HBM = pl.BlockSpec(memory_space=pltpu.HBM)


def call(kernel, name, specs, out_shapes, scratch, copies, mib=32, cost=None):
    if copies:
        scratch = scratch + [pltpu.SemaphoreType.DMA((copies,))]
    return pl.pallas_call(
        kernel,
        in_specs=specs,
        out_specs=[pl.BlockSpec(memory_space=space) for space, _ in out_shapes],
        out_shape=[
            pltpu.HBM(shape, BF16) if space is pltpu.HBM else jax.ShapeDtypeStruct(shape, BF16)
            for space, shape in out_shapes
        ],
        scratch_shapes=scratch,
        compiler_params=pltpu.CompilerParams(vmem_limit_bytes=mib * 1024 * 1024),
        cost_estimate=cost,
        name=name,
    )


def hbm(x):
    return pltpu.with_memory_space_constraint(x, pltpu.HBM)


def vmem(*shape):
    return pltpu.VMEM(shape, BF16)


def pick(first, a, b, axis):
    return jnp.where(first, jnp.concatenate([a, b], axis), jnp.concatenate([b, a], axis))


def per_device(tokens, space_gain, spatial_project, spatial_output, time_gain, temporal_project):
    core = lax.axis_index("core")
    x_lo = lax.axis_index("x_lo")
    x_hi = lax.axis_index("x_hi")
    tm = lax.axis_index(TM)
    swap = [(0, 1), (1, 0)]
    space_order = jnp.asarray(one_hot((16, 16, 6), (1, 0, 2)))
    inner_order = jnp.asarray(one_hot((16, 16, 3), (1, 0, 2)))
    time_order = jnp.asarray(one_hot((16, 4, 2, 2, 6), (1, 2, 3, 0, 4)))

    (chunk,) = call(
        chunk_kernel,
        "weight_rows",
        [SMEM] + [VMEM] * 3,
        [(pltpu.VMEM, (8, 2, 48, HALF))],
        [],
        0,
        12,
    )(tm.reshape(1).astype(jnp.int32), spatial_project, spatial_output, temporal_project)
    chunk = chunk.reshape(16, 48, HALF)
    got = lax.all_to_all(chunk, DP, 0, 0, tiled=True)
    across = lax.ppermute(tokens, "x_hi", swap)

    def moved(block):
        return lax.ppermute(
            lax.dynamic_index_in_dim(block, 1 - core, 1, keepdims=False), "core", swap
        )

    core_id = core.reshape(1).astype(jnp.int32)
    xh_id = x_hi.reshape(1).astype(jnp.int32)
    gain = space_gain.reshape(1, WIDTH)
    halves = tokens.reshape(4, 2, 32, WIDTH)
    frames, own = call(
        own_kernel,
        "space_norm_own",
        [SMEM] + [VMEM] * 3 + [HBM],
        [(pltpu.HBM, (8, 32, WIDTH)), (pltpu.HBM, (8, 1, 32, WIDTH))],
        [vmem(8, 32, WIDTH), vmem(8, 1, 32, WIDTH), vmem(WIDTH, WIDTH)],
        3,
        20,
        cost=pl.CostEstimate(flops=1, bytes_accessed=1, transcendentals=0),
    )(core_id, halves, moved(halves), gain, hbm(space_order))
    across, own = lax.optimization_barrier((across, own))
    halves = across.reshape(4, 2, 32, WIDTH)
    (normed,) = call(
        other_kernel,
        "space_norm_other",
        [SMEM] * 2 + [VMEM] * 3 + [HBM] * 2,
        [(pltpu.VMEM, (8, 2, 32, WIDTH))],
        [vmem(8, 32, WIDTH), vmem(4, WIDTH, HALF)],
        5,
        20,
    )(core_id, xh_id, halves, moved(halves), gain, hbm(own), hbm(space_order))
    got, normed = lax.optimization_barrier((got, normed))
    w1 = jnp.concatenate(
        [
            got[:, :12].reshape(16, 4, 3, HALF).transpose(1, 0, 2, 3).reshape(192, HALF),
            got[:, 12:30].reshape(16, 3, 6, HALF).transpose(1, 0, 2, 3).reshape(288, HALF),
        ],
        0,
    )
    w2 = got[:, 30:].reshape(16, 3, 6, HALF).transpose(1, 0, 2, 3).reshape(3, 1, 96, HALF)
    w2 = pick(x_hi == 0, w2, lax.ppermute(w2, "x_hi", swap), 1).reshape(576, HALF)
    w1 = lax.all_gather(w1, TM, axis=0, tiled=False)
    (tokens_time,) = call(
        tokens_kernel,
        "time_tokens",
        [HBM] * 2,
        [(pltpu.HBM, (256, WIDTH))],
        [vmem(256, WIDTH), vmem(WIDTH, WIDTH), vmem(256, WIDTH)],
        3,
        16,
    )(hbm(frames.reshape(256, WIDTH)), hbm(time_order))
    frame = lax.all_to_all(
        normed.reshape(8, 64, WIDTH), "z", 0, 0, axis_index_groups=[list(PLANES)], tiled=True
    )
    w2, frame, tokens_time = lax.optimization_barrier((w2, frame, tokens_time))
    w2 = lax.all_gather(w2, TM[1:], axis=0, tiled=False)
    frame = frame.reshape(512, WIDTH)
    (kv,) = call(
        keys_values_kernel,
        "space_keys_values",
        [VMEM, HBM],
        [(pltpu.VMEM, (2, 512, HALF))],
        [vmem(2, 16, 96, HALF)],
        2,
        24,
    )(frame, hbm(w1))
    kvo = lax.ppermute(kv, "core", swap)
    frame, kv = lax.optimization_barrier((frame, kv))
    (q,) = call(
        queries_kernel,
        "space_queries",
        [VMEM, HBM],
        [(pltpu.VMEM, (512, HALF))],
        [vmem(16, 96, HALF)],
        1,
        16,
    )(frame, hbm(w1))
    (ctx,) = call(spatial_kernel, "space_attend", [VMEM] * 3, [(pltpu.VMEM, (2, 8, 32, HALF))], [], 0, 20)(
        q, kv, kvo
    )
    w1, ctx = lax.optimization_barrier((w1, ctx))
    plain, mixed = call(
        weights_kernel,
        "output_weights",
        [HBM] * 3,
        [(pltpu.HBM, (INNER, WIDTH)), (pltpu.HBM, (4, INNER, HALF))],
        [
            vmem(16, 192, HALF),
            vmem(INNER, INNER),
            vmem(WIDTH, WIDTH),
            vmem(INNER, WIDTH),
            vmem(4, INNER, HALF),
        ],
        8,
        24,
        cost=pl.CostEstimate(flops=5_400_000_000, bytes_accessed=15_000_000, transcendentals=0),
    )(hbm(w1), hbm(inner_order), hbm(time_order))
    gain = time_gain.reshape(16, 4, 2, 2, 6).transpose(1, 2, 3, 0, 4).reshape(1, WIDTH)
    ctx = lax.all_to_all(ctx.reshape(16, 32, HALF), DP[::-1], 0, 0, tiled=True)
    ctx = ctx.reshape(2, 256, HALF)
    (normed_time,) = call(
        output_kernel,
        "space_output",
        [VMEM, HBM, HBM, VMEM],
        [(pltpu.HBM, (2, 256, WIDTH))],
        [vmem(4, INNER, HALF), vmem(256, WIDTH), vmem(4, 256, HALF)],
        13,
        20,
    )(ctx, hbm(tokens_time), hbm(mixed), gain)
    ctx, normed_time = lax.optimization_barrier((ctx, normed_time))
    (branch,) = call(
        branch_kernel,
        "space_branch",
        [VMEM, HBM],
        [(pltpu.VMEM, (256, WIDTH))],
        [vmem(INNER, WIDTH)],
        1,
        12,
    )(ctx, hbm(plain))
    branch = branch.reshape(8, 32, WIDTH)
    mine = lax.dynamic_slice_in_dim(branch, core * 4, 4, 0)
    theirs = lax.dynamic_slice_in_dim(branch, (1 - core) * 4, 4, 0)
    back = lax.ppermute(theirs, "core", swap)
    branch = pick(core == 0, mine[:, None], back[:, None], 1).reshape(tokens.shape)

    columns = lax.all_to_all(normed_time.reshape(8, 64, WIDTH), TM[:2], 0, 0, tiled=True)
    (context,) = call(
        temporal_kernel,
        "time_attend",
        [VMEM, HBM],
        [(pltpu.VMEM, (16, 2, 16, HALF))],
        [vmem(3, 8, 192, HALF)],
        3,
    )(columns.reshape(512, WIDTH), hbm(w2))
    context = lax.all_to_all(context.reshape(16, 32, HALF), TM, 0, 0, tiled=True)
    context = context.reshape(2, 4, 2, 2, 2, 8, HALF).transpose(3, 4, 2, 1, 5, 0, 6)
    return branch, context.reshape(2, 2, 64, INNER)


def solution(mesh):
    fine = Mesh(mesh.devices.reshape(2, 4, 2, 8, 2), TM + DP)
    in_specs = (P(None, TM, DP, None), P(), P(DP, None), P(DP, None), P(), P(DP, None))
    out_specs = (P(None, TM, DP, None), P(None, TM, DP, None))
    return jax.shard_map(
        per_device, mesh=fine, in_specs=in_specs, out_specs=out_specs, check_vma=False
    )
```

```python
import functools
import math

import jax
import jax.numpy as jnp
import numpy as np
from jax import lax
from jax.experimental import pallas as pl
from jax.experimental.pallas import tpu as pltpu
from jax.sharding import Mesh
from jax.sharding import PartitionSpec as P

HEADS = 8
HSIZE = 96
WIDTH = 1536
INNER = 768
HALF = INNER // 2
EPSILON = 1e-05
SCALE = math.log2(math.e) / math.sqrt(HSIZE)
TM = ("x_lo", "y", "core")
DP = ("z", "x_hi")
PLANES = (0, 4, 2, 6, 1, 5, 3, 7)
SHARDS = [2 * z + x for z in PLANES for x in range(2)]
BF16 = jnp.bfloat16
F32 = jnp.float32


def dot(a, b):
    return jnp.dot(a, b, preferred_element_type=F32)


def dot_nt(a, b):
    return lax.dot_general(a, b, (((1,), (1,)), ((), ())), preferred_element_type=F32)


def one_hot(shape, order):
    size = math.prod(shape)
    source = np.arange(size).reshape(shape)[SHARDS].transpose(order).reshape(-1)
    return (np.arange(size)[:, None] == source[None]).astype(jnp.bfloat16)


def fetch(pairs, sems):
    copies = [pltpu.make_async_copy(a, b, sems.at[i]) for i, (a, b) in enumerate(pairs)]
    for copy in copies:
        copy.start()
    return copies


def chunk_kernel(tm_ref, wq_ref, wo_ref, wt_ref, out_ref):
    tm = tm_ref[0]
    half = pl.multiple_of(tm // 8 * HALF, HALF)
    for h in range(2):
        pieces = [(wo_ref[:, cb * HALF : (cb + 1) * HALF], 3 * cb, 3, tm * 3) for cb in range(4)]
        for kind in range(3):
            first = kind * INNER + h * HALF
            pieces.append((wq_ref[:, first : first + HALF], 12 + 6 * kind, 6, tm * 6))
            lanes = pl.ds(pl.multiple_of(kind * INNER + half, HALF), HALF)
            pieces.append((wt_ref[:, lanes], 30 + 6 * kind, 6, tm % 8 * 12 + h * 6))
        total = jnp.zeros((48, HALF), F32)
        for block, place, count, source in pieces:
            row = lax.broadcasted_iota(jnp.int32, (48, block.shape[0]), 0) - place
            column = lax.broadcasted_iota(jnp.int32, (48, block.shape[0]), 1) - source
            picked = (row == column) & (row >= 0) & (row < count)
            total += dot(picked.astype(BF16), block)
        for z in range(8):
            out_ref[z, h] = total.astype(BF16)


def gather_frames(core, block_ref, moved_ref, frames_vmem):
    frames_vmem[pl.ds(core * 4, 4)] = block_ref[:, pl.ds(core, 1)].reshape(4, 32, WIDTH)
    frames_vmem[pl.ds((1 - core) * 4, 4)] = moved_ref[...]


def normalize(frames_vmem, gain_ref):
    x = frames_vmem[...].reshape(256, WIDTH).astype(F32)
    factor = lax.rsqrt(jnp.mean(x * x, axis=-1, keepdims=True) + EPSILON)
    return (x * factor * gain_ref[...]).astype(BF16)


def own_kernel(
    core_ref, block_ref, moved_ref, gain_ref, order_ref,
    frames_ref, out_ref, frames_vmem, out_vmem, order_vmem, sems,
):
    copies = fetch([(order_ref, order_vmem)], sems)
    gather_frames(core_ref[0], block_ref, moved_ref, frames_vmem)
    copies += fetch([(frames_vmem, frames_ref)], sems.at[pl.ds(1, 1)])
    normed = normalize(frames_vmem, gain_ref)
    copies[0].wait()
    out_vmem[...] = dot(normed, order_vmem[...]).astype(BF16).reshape(8, 1, 32, WIDTH)
    copies += fetch([(out_vmem, out_ref)], sems.at[pl.ds(2, 1)])
    copies[1].wait()
    copies[2].wait()


def other_kernel(
    core_ref, xh_ref, block_ref, moved_ref, gain_ref, own_ref, order_ref,
    out_ref, frames_vmem, order_vmem, sems,
):
    xh = xh_ref[0]
    pairs = [
        (order_ref.at[:, pl.ds(cb * HALF, HALF)], order_vmem.at[cb]) for cb in range(4)
    ]
    copies = fetch(pairs + [(own_ref, out_ref.at[:, pl.ds(xh, 1)])], sems)
    gather_frames(core_ref[0], block_ref, moved_ref, frames_vmem)
    normed = normalize(frames_vmem, gain_ref)
    for cb in range(4):
        copies[cb].wait()
        other = dot(normed, order_vmem[cb]).astype(BF16).reshape(8, 1, 32, HALF)
        out_ref[:, pl.ds(1 - xh, 1), :, cb * HALF : (cb + 1) * HALF] = other
    copies[4].wait()


def keys_values_kernel(x_ref, w_ref, kv_ref, w_vmem, sems):
    copies = fetch(
        [(w_ref.at[:, pl.ds(192 + 96 * i, 96)], w_vmem.at[i - 1]) for i in (1, 2)], sems
    )
    for i in range(2):
        copies[i].wait()
        kv_ref[i] = dot(x_ref[...], w_vmem[i].reshape(WIDTH, HALF)).astype(BF16)


def queries_kernel(x_ref, w_ref, q_ref, w_vmem, sems):
    fetch([(w_ref.at[:, pl.ds(192, 96)], w_vmem)], sems)[0].wait()
    q_ref[...] = dot(x_ref[...], w_vmem[...].reshape(WIDTH, HALF)).astype(BF16)


def attend(queries, keys, values, mask=None):
    outs = []
    for h, (first, last) in enumerate(((0, 128), (0, 256), (128, 384), (256, 384))):
        lane = lax.broadcasted_iota(jnp.int32, (1, last - first), 1) + first
        head = (lane >= h * HSIZE) & (lane < (h + 1) * HSIZE)
        q = jnp.where(head, queries[:, first:last], jnp.zeros((), BF16))
        scores = [dot_nt(q, k[:, first:last]) for k in keys]
        if mask is not None:
            scores = [jnp.where(mask, s, -jnp.inf) for s in scores]
        peak = functools.reduce(
            jnp.maximum, [jnp.max(s, axis=-1, keepdims=True) for s in scores]
        )
        terms = [jnp.exp2((s - peak) * SCALE) for s in scores]
        summed = sum(jnp.sum(t, axis=-1, keepdims=True) for t in terms)
        acc = sum(dot(t.astype(BF16), v[:, first:last]) for t, v in zip(terms, values))
        outs.append(acc * (1.0 / summed))
    lane = lax.broadcasted_iota(jnp.int32, (1, 128), 1)
    return (
        jnp.where(lane < 96, outs[0], outs[1][:, :128]),
        jnp.where(lane < 64, outs[1][:, 128:], outs[2][:, :128]),
        jnp.where(lane < 32, outs[2][:, 128:], outs[3]),
    )


def spatial_kernel(q_ref, kv_ref, kvo_ref, out_ref):
    for first in (0, 256):
        rows = slice(first, first + 256)
        blocks = attend(q_ref[rows], (kv_ref[0], kvo_ref[0]), (kv_ref[1], kvo_ref[1]))
        for i, block in enumerate(blocks):
            block = block.astype(BF16).reshape(4, 2, 32, 128)
            for k in range(4):
                z = PLANES[first // 64 + k]
                for xh in range(2):
                    out_ref[xh, z, :, i * 128 : (i + 1) * 128] = block[k, xh]


def weights_kernel(
    w_ref, inner_ref, time_ref,
    plain_ref, mixed_ref, w_vmem, inner_vmem, time_vmem, plain_vmem, mixed_vmem, sems,
):
    copies = fetch(
        [
            (inner_ref, inner_vmem),
            (w_ref.at[:, pl.ds(0, 192)], w_vmem),
            (time_ref, time_vmem),
        ],
        sems,
    )
    copies[0].wait()
    copies[1].wait()
    for cb in range(4):
        w = w_vmem[:, cb * 48 : (cb + 1) * 48, :].reshape(INNER, HALF)
        plain_vmem[:, cb * HALF : (cb + 1) * HALF] = dot(inner_vmem[...], w).astype(BF16)
    copies[2].wait()
    out = fetch([(plain_vmem, plain_ref)], sems.at[pl.ds(3, 1)])
    for cb in range(4):
        lanes = slice(cb * HALF, (cb + 1) * HALF)
        mixed_vmem[cb] = dot(plain_vmem[...], time_vmem[:, lanes]).astype(BF16)
        out += fetch([(mixed_vmem.at[cb], mixed_ref.at[cb])], sems.at[pl.ds(4 + cb, 1)])
    for copy in out:
        copy.wait()


def tokens_kernel(tok_ref, time_ref, out_ref, tok_vmem, time_vmem, out_vmem, sems):
    for copy in fetch([(tok_ref, tok_vmem), (time_ref, time_vmem)], sems):
        copy.wait()
    out_vmem[...] = dot(tok_vmem[...], time_vmem[...]).astype(BF16)
    fetch([(out_vmem, out_ref)], sems.at[pl.ds(2, 1)])[0].wait()


def join(ctx_ref):
    rows = [
        jnp.concatenate([ctx_ref[i, 32 * z : 32 * z + 32] for z in PLANES], axis=0)
        for i in range(2)
    ]
    return jnp.concatenate(rows, axis=1)


def output_kernel(
    ctx_ref, tok_ref, w_ref, gain_ref, out_ref, w_vmem, tok_vmem, out_vmem, sems
):
    copies = fetch(
        [(w_ref.at[cb], w_vmem.at[cb]) for cb in range(4)] + [(tok_ref, tok_vmem)], sems
    )
    rows = tok_ref.shape[0]
    ctx = join(ctx_ref)
    target = lax.broadcasted_iota(jnp.int32, (rows, rows), 0)
    source = (target % 64) // 8 * 32 + target // 64 * 8 + target % 8
    swap = (lax.broadcasted_iota(jnp.int32, (rows, rows), 1) == source).astype(BF16)
    branches = []
    for cb in range(4):
        copies[cb].wait()
        branches.append(dot(ctx, w_vmem[cb]).astype(BF16))
    copies[4].wait()
    mixed = []
    total = jnp.zeros((rows, 1), F32)
    for cb, branch in enumerate(branches):
        mix = tok_vmem[:, cb * HALF : (cb + 1) * HALF].astype(F32) + branch.astype(F32)
        mixed.append(mix)
        total += jnp.sum(mix * mix, axis=-1, keepdims=True)
    factor = lax.rsqrt(total * (1.0 / WIDTH) + EPSILON)
    for cb, mix in enumerate(mixed):
        lanes = slice(cb * HALF, (cb + 1) * HALF)
        normed = (mix * factor * gain_ref[:, lanes]).astype(BF16)
        out_vmem[cb] = dot(swap, normed).astype(BF16)
        for i in range(2):
            place = out_ref.at[i, :, pl.ds(cb * HALF, HALF)]
            copies += fetch([(out_vmem.at[cb], place)], sems.at[pl.ds(5 + 2 * cb + i, 1)])
    for copy in copies[5:]:
        copy.wait()


def branch_kernel(ctx_ref, w_ref, out_ref, w_vmem, sems):
    copies = fetch([(w_ref, w_vmem)], sems)
    ctx = join(ctx_ref)
    copies[0].wait()
    for cb in range(4):
        lanes = slice(cb * HALF, (cb + 1) * HALF)
        out_ref[:, lanes] = dot(ctx, w_vmem[:, lanes]).astype(BF16)


def temporal_kernel(x_ref, w_ref, out_ref, w_vmem, sems):
    copies = fetch([(w_ref.at[:, pl.ds(192 * i, 192)], w_vmem.at[i]) for i in range(3)], sems)
    r = lax.broadcasted_iota(jnp.int32, (256, 256), 0)
    s = lax.broadcasted_iota(jnp.int32, (256, 256), 1)
    mask = (r % 8 == s % 8) & (r // 8 >= s // 8)
    parts = []
    for i in range(3):
        copies[i].wait()
        part = dot(x_ref[...], w_vmem[i].reshape(WIDTH, HALF)).astype(BF16)
        parts.append(part.reshape(16, 2, 16, HALF))
    for history in range(2):
        query, key, value = (part[:, history].reshape(256, HALF) for part in parts)
        for i, block in enumerate(attend(query, (key,), (value,), mask)):
            block = block.astype(BF16).reshape(16, 16, 128)
            out_ref[:, history, :, i * 128 : (i + 1) * 128] = block


SMEM = pl.BlockSpec(memory_space=pltpu.SMEM)
VMEM = pl.BlockSpec(memory_space=pltpu.VMEM)
HBM = pl.BlockSpec(memory_space=pltpu.HBM)


def call(kernel, name, specs, out_shapes, scratch, copies, mib=32, cost=None):
    if copies:
        scratch = scratch + [pltpu.SemaphoreType.DMA((copies,))]
    return pl.pallas_call(
        kernel,
        in_specs=specs,
        out_specs=[pl.BlockSpec(memory_space=space) for space, _ in out_shapes],
        out_shape=[
            pltpu.HBM(shape, BF16) if space is pltpu.HBM else jax.ShapeDtypeStruct(shape, BF16)
            for space, shape in out_shapes
        ],
        scratch_shapes=scratch,
        compiler_params=pltpu.CompilerParams(vmem_limit_bytes=mib * 1024 * 1024),
        cost_estimate=cost,
        name=name,
    )


def hbm(x):
    return pltpu.with_memory_space_constraint(x, pltpu.HBM)


def vmem(*shape):
    return pltpu.VMEM(shape, BF16)


def pick(first, a, b, axis):
    return jnp.where(first, jnp.concatenate([a, b], axis), jnp.concatenate([b, a], axis))


def per_device(tokens, space_gain, spatial_project, spatial_output, time_gain, temporal_project):
    core = lax.axis_index("core")
    x_lo = lax.axis_index("x_lo")
    x_hi = lax.axis_index("x_hi")
    tm = lax.axis_index(TM)
    swap = [(0, 1), (1, 0)]
    space_order = jnp.asarray(one_hot((16, 16, 6), (1, 0, 2)))
    inner_order = jnp.asarray(one_hot((16, 16, 3), (1, 0, 2)))
    time_order = jnp.asarray(one_hot((16, 4, 2, 2, 6), (1, 2, 3, 0, 4)))

    (chunk,) = call(
        chunk_kernel,
        "weight_rows",
        [SMEM] + [VMEM] * 3,
        [(pltpu.VMEM, (8, 2, 48, HALF))],
        [],
        0,
        12,
    )(tm.reshape(1).astype(jnp.int32), spatial_project, spatial_output, temporal_project)
    chunk = chunk.reshape(16, 48, HALF)
    got = lax.all_to_all(chunk, DP, 0, 0, axis_index_groups=[SHARDS], tiled=True)
    across = lax.ppermute(tokens, "x_hi", swap)

    def moved(block):
        return lax.ppermute(
            lax.dynamic_index_in_dim(block, 1 - core, 1, keepdims=False), "core", swap
        )

    core_id = core.reshape(1).astype(jnp.int32)
    xh_id = x_hi.reshape(1).astype(jnp.int32)
    gain = space_gain.reshape(1, WIDTH)
    halves = tokens.reshape(4, 2, 32, WIDTH)
    frames, own = call(
        own_kernel,
        "space_norm_own",
        [SMEM] + [VMEM] * 3 + [HBM],
        [(pltpu.HBM, (8, 32, WIDTH)), (pltpu.HBM, (8, 1, 32, WIDTH))],
        [vmem(8, 32, WIDTH), vmem(8, 1, 32, WIDTH), vmem(WIDTH, WIDTH)],
        3,
        20,
        cost=pl.CostEstimate(flops=1, bytes_accessed=1, transcendentals=0),
    )(core_id, halves, moved(halves), gain, hbm(space_order))
    across, own = lax.optimization_barrier((across, own))
    halves = across.reshape(4, 2, 32, WIDTH)
    (normed,) = call(
        other_kernel,
        "space_norm_other",
        [SMEM] * 2 + [VMEM] * 3 + [HBM] * 2,
        [(pltpu.VMEM, (8, 2, 32, WIDTH))],
        [vmem(8, 32, WIDTH), vmem(4, WIDTH, HALF)],
        5,
        20,
    )(core_id, xh_id, halves, moved(halves), gain, hbm(own), hbm(space_order))
    got, normed = lax.optimization_barrier((got, normed))
    w1 = jnp.concatenate(
        [
            got[:, :12].reshape(16, 4, 3, HALF).transpose(1, 0, 2, 3).reshape(192, HALF),
            got[:, 12:30].reshape(16, 3, 6, HALF).transpose(1, 0, 2, 3).reshape(288, HALF),
        ],
        0,
    )
    w2 = got[:, 30:].reshape(16, 3, 6, HALF).transpose(1, 0, 2, 3).reshape(3, 1, 96, HALF)
    w2 = pick(x_hi == 0, w2, lax.ppermute(w2, "x_hi", swap), 1).reshape(576, HALF)
    w1 = lax.all_gather(w1, TM, axis=0, tiled=False)
    (tokens_time,) = call(
        tokens_kernel,
        "time_tokens",
        [HBM] * 2,
        [(pltpu.HBM, (256, WIDTH))],
        [vmem(256, WIDTH), vmem(WIDTH, WIDTH), vmem(256, WIDTH)],
        3,
        16,
    )(hbm(frames.reshape(256, WIDTH)), hbm(time_order))
    frame = lax.all_to_all(
        normed.reshape(8, 64, WIDTH), "z", 0, 0, axis_index_groups=[list(PLANES)], tiled=True
    )
    w2, frame, tokens_time = lax.optimization_barrier((w2, frame, tokens_time))
    w2 = lax.all_gather(w2, TM[1:], axis=0, tiled=False)
    frame = frame.reshape(512, WIDTH)
    (kv,) = call(
        keys_values_kernel,
        "space_keys_values",
        [VMEM, HBM],
        [(pltpu.VMEM, (2, 512, HALF))],
        [vmem(2, 16, 96, HALF)],
        2,
        24,
    )(frame, hbm(w1))
    kvo = lax.ppermute(kv, "core", swap)
    frame, kv = lax.optimization_barrier((frame, kv))
    (q,) = call(
        queries_kernel,
        "space_queries",
        [VMEM, HBM],
        [(pltpu.VMEM, (512, HALF))],
        [vmem(16, 96, HALF)],
        1,
        16,
    )(frame, hbm(w1))
    (ctx,) = call(spatial_kernel, "space_attend", [VMEM] * 3, [(pltpu.VMEM, (2, 8, 32, HALF))], [], 0, 20)(
        q, kv, kvo
    )
    w1, ctx = lax.optimization_barrier((w1, ctx))
    plain, mixed = call(
        weights_kernel,
        "output_weights",
        [HBM] * 3,
        [(pltpu.HBM, (INNER, WIDTH)), (pltpu.HBM, (4, INNER, HALF))],
        [
            vmem(16, 192, HALF),
            vmem(INNER, INNER),
            vmem(WIDTH, WIDTH),
            vmem(INNER, WIDTH),
            vmem(4, INNER, HALF),
        ],
        8,
        24,
        cost=pl.CostEstimate(flops=5_400_000_000, bytes_accessed=15_000_000, transcendentals=0),
    )(hbm(w1), hbm(inner_order), hbm(time_order))
    gain = time_gain.reshape(16, 4, 2, 2, 6)
    gain = jnp.concatenate([gain[d : d + 1] for d in SHARDS]).transpose(1, 2, 3, 0, 4).reshape(1, WIDTH)
    ctx = lax.all_to_all(ctx.reshape(16, 32, HALF), DP[::-1], 0, 0, tiled=True)
    ctx = ctx.reshape(2, 256, HALF)
    (normed_time,) = call(
        output_kernel,
        "space_output",
        [VMEM, HBM, HBM, VMEM],
        [(pltpu.HBM, (2, 256, WIDTH))],
        [vmem(4, INNER, HALF), vmem(256, WIDTH), vmem(4, 256, HALF)],
        13,
        20,
    )(ctx, hbm(tokens_time), hbm(mixed), gain)
    ctx, normed_time = lax.optimization_barrier((ctx, normed_time))
    (branch,) = call(
        branch_kernel,
        "space_branch",
        [VMEM, HBM],
        [(pltpu.VMEM, (256, WIDTH))],
        [vmem(INNER, WIDTH)],
        1,
        12,
    )(ctx, hbm(plain))
    branch = branch.reshape(8, 32, WIDTH)
    mine = lax.dynamic_slice_in_dim(branch, core * 4, 4, 0)
    theirs = lax.dynamic_slice_in_dim(branch, (1 - core) * 4, 4, 0)
    back = lax.ppermute(theirs, "core", swap)
    branch = pick(core == 0, mine[:, None], back[:, None], 1).reshape(tokens.shape)

    columns = lax.all_to_all(normed_time.reshape(8, 64, WIDTH), TM[:2], 0, 0, tiled=True)
    (context,) = call(
        temporal_kernel,
        "time_attend",
        [VMEM, HBM],
        [(pltpu.VMEM, (16, 2, 16, HALF))],
        [vmem(3, 8, 192, HALF)],
        3,
    )(columns.reshape(512, WIDTH), hbm(w2))
    context = lax.all_to_all(context.reshape(16, 32, HALF), TM, 0, 0, tiled=True)
    context = context.reshape(2, 4, 2, 2, 2, 8, HALF).transpose(3, 4, 2, 1, 5, 0, 6)
    return branch, context.reshape(2, 2, 64, INNER)


def solution(mesh):
    fine = Mesh(mesh.devices.reshape(2, 4, 2, 8, 2), TM + DP)
    in_specs = (P(None, TM, DP, None), P(), P(DP, None), P(DP, None), P(), P(DP, None))
    out_specs = (P(None, TM, DP, None), P(None, TM, DP, None))
    return jax.shard_map(
        per_device, mesh=fine, in_specs=in_specs, out_specs=out_specs, check_vma=False
    )
```
